512 devices in a mesh: grp: 16 (over y, z_hi), row: 32 (over z_lo, x, core).
Axes of the slice: x: 4, y: 4, z: 16 (z_hi: 4, z_lo: 4; z = z_hi * 4 + z_lo), core: 2. Of those that a mesh axis runs over, the one named last changes fastest.
Arguments:
- integrals: bfloat16 [16, 6144, 6144], P('grp', 'row'), may hold values from -6 to 6
- occupied: bfloat16 [6144, 512], P('row'), may hold values from -0.0078125 to 0.0078125
Outputs:
- exchange_matrix: float32 [6144, 6144], P('row', 'grp')
The draws below stay inside these ranges and needn't reach their ends.
All inputs are finite; a program needn't handle non-finite values.
Results may differ from the reference program's by a relative error of at most 0.015.
Values may be sent and summed in bfloat16 or wider, within the bound.
A program may use at most 64 MiB of HBM per device.

```python
import jax
import jax.numpy as jnp
from jax import lax

NBAS = 6144
NOCC = 512
AUX_G = 1
AUX = 16
N_GRP = 16


def block_scale(own_key, extent, split, least, high):
    factor_of = 1.0
    for position, shards_of in split:
        draws = jax.random.uniform(jax.random.fold_in(jax.random.fold_in(own_key, 6), position), (shards_of,), jnp.float32, least / len(split), high / len(split))
        factor_of = factor_of * jnp.repeat(jnp.exp(draws), extent[position] // shards_of).reshape((-1,) + (1,) * (len(extent) - 1 - position))
    return factor_of


def noise(own_key, extent, width, limit, split=(), kind=jnp.bfloat16):
    entries = jax.random.normal(own_key, extent, jnp.float32) * width
    if len(split) > 0:
        entries = block_scale(own_key, extent, split, -0.22, 0.18) * entries
    return jnp.clip(entries, min=-limit, max=limit).astype(kind)


def setup_inputs(seed: int = 0) -> dict:
    key_list = jax.random.split(jax.random.key(seed), 3)
    integrals = noise(key_list[0], (AUX, NBAS, NBAS), 1.0, 6.0, ((0, 16), (1, 32)))
    occupied = noise(key_list[1], (NBAS, NOCC), (NBAS * 96) ** -0.5, 0.0078125, ((0, 32),))
    return {"integrals": integrals, "occupied": occupied}


def reference(integrals, occupied):
    basis_width = integrals.shape[1]

    def group_step(running, group):
        pieces = []
        for member in range(AUX_G):
            matrix = lax.dynamic_index_in_dim(integrals, (group * AUX_G + member).astype(jnp.int32), 0, keepdims=False)
            pieces.append(jnp.dot(matrix, occupied, preferred_element_type=jnp.float32).astype(jnp.bfloat16))
        half_rows = jnp.concatenate(pieces, axis=1)
        partial_value = jnp.dot(half_rows, half_rows.T, preferred_element_type=jnp.float32).astype(jnp.bfloat16)
        return running + partial_value.astype(jnp.float32), None

    start_value = jnp.zeros((basis_width, basis_width), jnp.float32)
    result, ignored = lax.scan(group_step, start_value, jnp.arange(N_GRP, dtype=jnp.int32))
    return result
```

```python
import jax
import jax.numpy as jnp
from jax import lax
from jax.experimental import pallas as pl
from jax.experimental.pallas import tpu as pltpu
from jax.sharding import PartitionSpec as P

MESH = pl.DeviceIdType.MESH
F32 = jnp.float32
BF16 = jnp.bfloat16

N_SEM = 192


def kernel(ints_hbm, occ_hbm, out_ref, occ, ints, hacc, hrow, hcol, pb,
           yin, ysum, xin, zin, zbuf, ssem, rsem, lsem):
    grp, row = lax.axis_index("grp"), lax.axis_index("row")
    y, zh = grp // 4, grp % 4
    zl, x, c = row // 8, (row // 2) % 4, row % 2
    z = zh * 4 + zl

    def up(v, d, n=4):
        return (v + d + n) % n

    def at(dx=0, dy=0, dz=0):
        zz = up(z, dz, 16)
        return (up(y, dy) * 4 + zz // 4, (zz % 4) * 8 + up(x, dx) * 2 + c)

    def in_group(d):
        return (grp, up(zl, d) * 8 + x * 2 + c)

    sibling = (grp, zl * 8 + x * 2 + (1 - c))

    copies = []

    def send(src, dst, to):
        k = len(copies)
        copy = pltpu.make_async_remote_copy(
            src_ref=src, dst_ref=dst, send_sem=ssem.at[k], recv_sem=rsem.at[k],
            device_id=to, device_id_type=MESH)
        copy.start()
        copies.append(copy)
        return copy

    def same(ref, to):
        return send(ref, ref, to)

    own_copy = pltpu.make_async_copy(occ_hbm, occ.at[zl, x, c], lsem.at[0])
    own_copy.start()
    ints_copy = pltpu.make_async_copy(ints_hbm, ints, lsem.at[1])
    ints_copy.start()

    barrier = pltpu.get_barrier_semaphore()
    partners = [sibling, at(dx=1), at(dx=2), at(dx=-1), at(dy=1), at(dy=-1), at(dz=1), at(dz=-1),
                at(dz=4), at(dz=-4), in_group(1), in_group(2), in_group(3)]
    for partner in partners:
        pl.semaphore_signal(barrier, inc=1, device_id=partner, device_id_type=MESH)
    pl.semaphore_wait(barrier, len(partners))
    own_copy.wait()

    xr, xl, xo = up(x, 1), up(x, -1), up(x, 2)
    zr, zd, zo = up(zl, 1), up(zl, -1), up(zl, 2)
    east, west, north, south = at(dx=1), at(dx=-1), at(dz=1), at(dz=-1)
    PA, PB = pl.ds(0, 256), pl.ds(256, 256)
    ALL, TOP, BOT = pl.ds(0, 192), pl.ds(0, 96), pl.ds(96, 96)

    def blk(bz, bx, rows, cols):
        return occ.at[bz, bx, c, rows, cols]

    fwd_a = [[], []]
    fwd_b = [[], []]
    own_a, own_b = blk(zl, x, ALL, PA), blk(zl, x, ALL, PB)
    a_e, a_w = same(own_a, east), same(own_a, west)
    b_n, b_s = same(own_b, north), same(own_b, south)
    fwd_a[0].append(same(own_a, north))
    fwd_a[1].append(same(own_a, south))
    fwd_b[0].append(same(own_b, east))
    fwd_b[1].append(same(own_b, west))
    sib_own = same(occ.at[zl, x, c], sibling)

    a_e.wait_recv()
    a_et = same(blk(zl, xl, TOP, PA), east)
    fwd_a[0].append(same(blk(zl, xl, ALL, PA), north))
    fwd_a[1].append(same(blk(zl, xl, ALL, PA), south))
    b_n.wait_recv()
    b_nt = same(blk(zd, x, TOP, PB), north)
    fwd_b[0].append(same(blk(zd, x, ALL, PB), east))
    fwd_b[1].append(same(blk(zd, x, ALL, PB), west))
    a_w.wait_recv()
    a_wb = same(blk(zl, xr, BOT, PA), west)
    fwd_a[0].append(same(blk(zl, xr, ALL, PA), north))
    fwd_a[1].append(same(blk(zl, xr, ALL, PA), south))
    b_s.wait_recv()
    b_sb = same(blk(zr, x, BOT, PB), south)
    fwd_b[0].append(same(blk(zr, x, ALL, PB), east))
    fwd_b[1].append(same(blk(zr, x, ALL, PB), west))
    sib_a0 = [sib_own, same(blk(zl, xl, ALL, PA), sibling), same(blk(zl, xr, ALL, PA), sibling)]
    sib_b0 = [same(blk(zd, x, ALL, PB), sibling), same(blk(zr, x, ALL, PB), sibling)]
    a_et.wait_recv()
    a_wb.wait_recv()
    fwd_a[0].append(same(blk(zl, xo, ALL, PA), north))
    fwd_a[1].append(same(blk(zl, xo, ALL, PA), south))
    sib_a0.append(same(blk(zl, xo, ALL, PA), sibling))
    b_nt.wait_recv()
    b_sb.wait_recv()
    fwd_b[0].append(same(blk(zo, x, ALL, PB), east))
    fwd_b[1].append(same(blk(zo, x, ALL, PB), west))
    sib_b0.append(same(blk(zo, x, ALL, PB), sibling))

    last_a, last_b = [], []
    sib_a1, sib_b1 = [], []
    for bx, bz, j in zip((x, xl, xr, xo), (zl, zd, zr, zo), range(4)):
        fwd_a[0][j].wait_recv()
        t = same(blk(zd, bx, TOP, PA), north)
        sib_a1.append(same(blk(zd, bx, ALL, PA), sibling))
        fwd_a[1][j].wait_recv()
        u = same(blk(zr, bx, BOT, PA), south)
        sib_a1.append(same(blk(zr, bx, ALL, PA), sibling))
        last_a.append((t, u, bx))
        fwd_b[0][j].wait_recv()
        t = same(blk(bz, xl, TOP, PB), east)
        sib_b1.append(same(blk(bz, xl, ALL, PB), sibling))
        fwd_b[1][j].wait_recv()
        u = same(blk(bz, xr, BOT, PB), west)
        sib_b1.append(same(blk(bz, xr, ALL, PB), sibling))
        last_b.append((t, u, bz))

    def lanes(start, size):
        return pl.ds(pl.multiple_of(start, 128), size)

    def part_a(bz):
        return jnp.dot(ints[:, lanes(bz * 1536, 1536)],
                       occ[bz, :, :, :, 0:256].reshape(1536, 256), preferred_element_type=F32)

    def part_b(bx):
        total = None
        for bz in range(4):
            term = jnp.dot(ints[:, lanes(bz * 1536 + bx * 384, 384)],
                           occ[bz, bx, :, :, 256:512].reshape(384, 256), preferred_element_type=F32)
            total = term if total is None else total + term
        return total

    ints_copy.wait()
    for copy in sib_a0 + sib_b0:
        copy.wait_recv()
    hacc[:, 0:256] = part_a(zl)
    hacc[:, 256:512] = part_b(x)
    for copy in sib_a1 + sib_b1:
        copy.wait_recv()
    hacc[:, 0:256] += part_a(zd)
    hacc[:, 256:512] += part_b(xl)
    hacc[:, 0:256] += part_a(zr)
    hacc[:, 256:512] += part_b(xr)
    sib_2 = []
    for (t, u, bx), (v, w, bz) in zip(last_a, last_b):
        t.wait_recv()
        u.wait_recv()
        sib_2.append(same(blk(zo, bx, ALL, PA), sibling))
        v.wait_recv()
        w.wait_recv()
        sib_2.append(same(blk(bz, xo, ALL, PB), sibling))
    for copy in sib_2:
        copy.wait_recv()
    h_a = (hacc[:, 0:256] + part_a(zo)).astype(BF16)
    h_b = (hacc[:, 256:512] + part_b(xo)).astype(BF16)
    hrow[x, :, 0:256] = h_a
    hrow[x, :, 256:512] = h_b
    for s in range(3):
        hcol[s, zl, c, :, 0:256] = h_a[64 * s:64 * s + 64]
        hcol[s, zl, c, :, 256:512] = h_b[64 * s:64 * s + 64]

    r_e, r_w = same(hrow.at[x], east), same(hrow.at[x], west)
    c_in = []
    for s in range(3):
        c_in.append([same(hcol.at[s, zl, c], in_group(d)) for d in (1, 3, 2)])
    c_sib = [[same(hcol.at[s, zl, c], sibling)] for s in range(3)]
    r_e.wait_recv()
    r_et = same(hrow.at[xl, TOP], east)
    r_w.wait_recv()
    r_wb = same(hrow.at[xr, BOT], west)

    yr, yl, yo = up(y, 1), up(y, -1), up(y, 2)
    y_up, y_dn = at(dy=1), at(dy=-1)
    hr, hl, ho = up(zh, 1), up(zh, -1), up(zh, 2)
    z_up, z_dn = at(dz=4), at(dz=-4)
    A, B = pl.ds(0, 384), pl.ds(384, 384)
    TA, TB = pl.ds(0, 96), pl.ds(96, 96)
    y1, y2, xs, z1, z2 = {}, {}, {}, {}, {}

    def columns_in(s):
        for copy, d in zip(c_in[s], (3, 1, 2)):
            copy.wait_recv()
            c_sib[s].append(same(hcol.at[s, up(zl, d), c], sibling))
        for copy in c_sib[s]:
            copy.wait_recv()

    def product(s):
        for half in range(2):
            cols = hcol[s, 2 * half:2 * half + 2].reshape(256, 512)
            for bx in range(4):
                p = lax.dot_general(hrow[bx], cols, (((1,), (1,)), ((), ())), preferred_element_type=F32)
                p = p.astype(BF16)
                pb[s, 2 * half, 192 * bx:192 * bx + 192] = p[:, 0:128]
                pb[s, 2 * half + 1, 192 * bx:192 * bx + 192] = p[:, 128:256]

    def y_first(s):
        y1[s] = (send(pb.at[s, yo, A], yin.at[s, 0], y_up),
                 send(pb.at[s, yo, B], yin.at[s, 1], y_dn),
                 send(pb.at[s, yr, B], yin.at[s, 2], y_up),
                 send(pb.at[s, yl, A], yin.at[s, 3], y_dn))

    def y_second(s):
        y1[s][0].wait_recv()
        pb[s, yr, A] = (pb[s, yr, A].astype(F32) + yin[s, 0].astype(F32)).astype(BF16)
        up_copy = send(pb.at[s, yr, A], yin.at[s, 4], y_up)
        y1[s][1].wait_recv()
        pb[s, yl, B] = (pb[s, yl, B].astype(F32) + yin[s, 1].astype(F32)).astype(BF16)
        y2[s] = (up_copy, send(pb.at[s, yl, B], yin.at[s, 5], y_dn))

    def y_last(s):
        for copy in y1[s][2:] + y2[s]:
            copy.wait_recv()
        ysum[s, 0:2] = (pb[s, y, A].astype(F32) + yin[s, 3].astype(F32)
                        + yin[s, 4].astype(F32)).astype(BF16).reshape(2, 192, 128)
        ysum[s, 2:4] = (pb[s, y, B].astype(F32) + yin[s, 2].astype(F32)
                        + yin[s, 5].astype(F32)).astype(BF16).reshape(2, 192, 128)
        xs[s] = [send(ysum.at[s, up(x, d)], xin.at[s, x], at(dx=d)) for d in (2, 1, -1)]
        xin[s, x] = ysum[s, x]

    def z_first(s):
        for copy in xs[s]:
            copy.wait_recv()
        z1[s] = (send(xin.at[s, ho, TA], zin.at[s, 0], z_up),
                 send(xin.at[s, ho, TB], zin.at[s, 1], z_dn),
                 send(xin.at[s, hr, TB], zin.at[s, 2], z_up),
                 send(xin.at[s, hl, TA], zin.at[s, 3], z_dn))

    def z_second(s):
        z1[s][0].wait_recv()
        zbuf[s, 0] = (xin[s, hr, TA].astype(F32) + zin[s, 0].astype(F32)).astype(BF16)
        up_copy = send(zbuf.at[s, 0], zin.at[s, 4], z_up)
        z1[s][1].wait_recv()
        zbuf[s, 1] = (xin[s, hl, TB].astype(F32) + zin[s, 1].astype(F32)).astype(BF16)
        z2[s] = (up_copy, send(zbuf.at[s, 1], zin.at[s, 5], z_dn))

    def z_last(s):
        for copy in z1[s][2:] + z2[s]:
            copy.wait_recv()
        top = xin[s, zh, TA].astype(F32) + zin[s, 3].astype(F32) + zin[s, 4].astype(F32)
        bot = xin[s, zh, TB].astype(F32) + zin[s, 2].astype(F32) + zin[s, 5].astype(F32)
        for rows, v in ((slice(0, 96), top), (slice(96, 192), bot)):
            out_ref[rows, 64 * s:64 * s + 64] = v[:, 0:64]
            out_ref[rows, 192 + 64 * s:192 + 64 * s + 64] = v[:, 64:128]

    columns_in(0)
    r_et.wait_recv()
    r_wb.wait_recv()
    product(0)
    y_first(0)
    columns_in(1)
    product(1)
    y_second(0)
    y_first(1)
    columns_in(2)
    product(2)
    y_second(1)
    y_first(2)
    y_last(0)
    y_second(2)
    z_first(0)
    y_last(1)
    z_second(0)
    z_first(1)
    y_last(2)
    z_second(1)
    z_last(0)
    z_first(2)
    z_last(1)
    z_second(2)
    z_last(2)
    for copy in copies:
        copy.wait_send()


def local(integrals, occupied):
    return pl.pallas_call(
        kernel,
        out_shape=jax.ShapeDtypeStruct((192, 384), F32),
        in_specs=[pl.BlockSpec(memory_space=pl.ANY)] * 2,
        out_specs=pl.BlockSpec(memory_space=pltpu.VMEM),
        scratch_shapes=[
            pltpu.VMEM((4, 4, 2, 192, 512), BF16),
            pltpu.VMEM((192, 6144), BF16),
            pltpu.VMEM((192, 512), F32),
            pltpu.VMEM((4, 192, 512), BF16),
            pltpu.VMEM((3, 4, 2, 64, 512), BF16),
            pltpu.VMEM((3, 4, 768, 128), BF16),
            pltpu.VMEM((3, 6, 384, 128), BF16),
            pltpu.VMEM((3, 4, 192, 128), BF16),
            pltpu.VMEM((3, 4, 192, 128), BF16),
            pltpu.VMEM((3, 6, 96, 128), BF16),
            pltpu.VMEM((3, 2, 96, 128), BF16),
            pltpu.SemaphoreType.DMA((N_SEM,)),
            pltpu.SemaphoreType.DMA((N_SEM,)),
            pltpu.SemaphoreType.DMA((2,)),
        ],
        compiler_params=pltpu.CompilerParams(
            collective_id=0, has_side_effects=True, vmem_limit_bytes=48 << 20),
        name="exchange",
    )(integrals.reshape(192, 6144), occupied)


def solution(mesh):
    in_specs = (P("grp", "row", None), P("row", None))
    return jax.shard_map(local, mesh=mesh, in_specs=in_specs, out_specs=P("row", "grp"), check_vma=False)
```

```python
import jax
import jax.numpy as jnp
from jax import lax
from jax.experimental import pallas as pl
from jax.experimental.pallas import tpu as pltpu
from jax.sharding import PartitionSpec as P

MESH = pl.DeviceIdType.MESH
F32 = jnp.float32
BF16 = jnp.bfloat16

N_SEM = 192


def kernel(ints_hbm, occ_hbm, out_ref, occ, ints, hacc, hrow, hcol, pb,
           yin, ysum, xin, zin, zbuf, ssem, rsem, lsem):
    grp, row = lax.axis_index("grp"), lax.axis_index("row")
    y, zh = grp // 4, grp % 4
    zl, x, c = row // 8, (row // 2) % 4, row % 2
    z = zh * 4 + zl

    def up(v, d, n=4):
        return (v + d + n) % n

    def at(dx=0, dy=0, dz=0):
        zz = up(z, dz, 16)
        return (up(y, dy) * 4 + zz // 4, (zz % 4) * 8 + up(x, dx) * 2 + c)

    def in_group(d):
        return (grp, up(zl, d) * 8 + x * 2 + c)

    sibling = (grp, zl * 8 + x * 2 + (1 - c))

    copies = []

    def send(src, dst, to):
        k = len(copies)
        copy = pltpu.make_async_remote_copy(
            src_ref=src, dst_ref=dst, send_sem=ssem.at[k], recv_sem=rsem.at[k],
            device_id=to, device_id_type=MESH)
        copy.start()
        copies.append(copy)
        return copy

    def same(ref, to):
        return send(ref, ref, to)

    own_copy = pltpu.make_async_copy(occ_hbm, occ.at[zl, x, c], lsem.at[0])
    own_copy.start()
    ints_copy = pltpu.make_async_copy(ints_hbm, ints, lsem.at[1])
    ints_copy.start()

    barrier = pltpu.get_barrier_semaphore()
    partners = [sibling, at(dx=1), at(dx=2), at(dx=-1), at(dy=1), at(dy=-1), at(dz=1), at(dz=-1),
                at(dz=4), at(dz=-4), in_group(1), in_group(2), in_group(3)]
    for partner in partners:
        pl.semaphore_signal(barrier, inc=1, device_id=partner, device_id_type=MESH)
    pl.semaphore_wait(barrier, len(partners))
    own_copy.wait()

    xr, xl, xo = up(x, 1), up(x, -1), up(x, 2)
    zr, zd, zo = up(zl, 1), up(zl, -1), up(zl, 2)
    east, west, north, south = at(dx=1), at(dx=-1), at(dz=1), at(dz=-1)
    PA, PB = pl.ds(0, 256), pl.ds(256, 256)
    ALL, TOP, BOT = pl.ds(0, 192), pl.ds(0, 96), pl.ds(96, 96)

    def blk(bz, bx, rows, cols):
        return occ.at[bz, bx, c, rows, cols]

    fwd_a = [[], []]
    fwd_b = [[], []]
    own_a, own_b = blk(zl, x, ALL, PA), blk(zl, x, ALL, PB)
    a_e, a_w = same(own_a, east), same(own_a, west)
    b_n, b_s = same(own_b, north), same(own_b, south)
    fwd_a[0].append(same(own_a, north))
    fwd_a[1].append(same(own_a, south))
    fwd_b[0].append(same(own_b, east))
    fwd_b[1].append(same(own_b, west))
    sib_own = same(occ.at[zl, x, c], sibling)

    a_e.wait_recv()
    a_et = same(blk(zl, xl, TOP, PA), east)
    fwd_a[0].append(same(blk(zl, xl, ALL, PA), north))
    fwd_a[1].append(same(blk(zl, xl, ALL, PA), south))
    b_n.wait_recv()
    b_nt = same(blk(zd, x, TOP, PB), north)
    fwd_b[0].append(same(blk(zd, x, ALL, PB), east))
    fwd_b[1].append(same(blk(zd, x, ALL, PB), west))
    a_w.wait_recv()
    a_wb = same(blk(zl, xr, BOT, PA), west)
    fwd_a[0].append(same(blk(zl, xr, ALL, PA), north))
    fwd_a[1].append(same(blk(zl, xr, ALL, PA), south))
    b_s.wait_recv()
    b_sb = same(blk(zr, x, BOT, PB), south)
    fwd_b[0].append(same(blk(zr, x, ALL, PB), east))
    fwd_b[1].append(same(blk(zr, x, ALL, PB), west))
    sib_a0 = [sib_own, same(blk(zl, xl, ALL, PA), sibling), same(blk(zl, xr, ALL, PA), sibling)]
    sib_b0 = [same(blk(zd, x, ALL, PB), sibling), same(blk(zr, x, ALL, PB), sibling)]
    a_et.wait_recv()
    a_wb.wait_recv()
    fwd_a[0].append(same(blk(zl, xo, ALL, PA), north))
    fwd_a[1].append(same(blk(zl, xo, ALL, PA), south))
    sib_a0.append(same(blk(zl, xo, ALL, PA), sibling))
    b_nt.wait_recv()
    b_sb.wait_recv()
    fwd_b[0].append(same(blk(zo, x, ALL, PB), east))
    fwd_b[1].append(same(blk(zo, x, ALL, PB), west))
    sib_b0.append(same(blk(zo, x, ALL, PB), sibling))

    last_a, last_b = [], []
    sib_a1, sib_b1 = [], []
    for bx, bz, j in zip((x, xl, xr, xo), (zl, zd, zr, zo), range(4)):
        fwd_a[0][j].wait_recv()
        t = same(blk(zd, bx, TOP, PA), north)
        sib_a1.append(same(blk(zd, bx, ALL, PA), sibling))
        fwd_a[1][j].wait_recv()
        u = same(blk(zr, bx, BOT, PA), south)
        sib_a1.append(same(blk(zr, bx, ALL, PA), sibling))
        last_a.append((t, u, bx))
        fwd_b[0][j].wait_recv()
        t = same(blk(bz, xl, TOP, PB), east)
        sib_b1.append(same(blk(bz, xl, ALL, PB), sibling))
        fwd_b[1][j].wait_recv()
        u = same(blk(bz, xr, BOT, PB), west)
        sib_b1.append(same(blk(bz, xr, ALL, PB), sibling))
        last_b.append((t, u, bz))

    def lanes(start, size):
        return pl.ds(pl.multiple_of(start, 128), size)

    def part_a(bz):
        return jnp.dot(ints[:, lanes(bz * 1536, 1536)],
                       occ[bz, :, :, :, 0:256].reshape(1536, 256), preferred_element_type=F32)

    def part_b(bx):
        total = None
        for bz in range(4):
            term = jnp.dot(ints[:, lanes(bz * 1536 + bx * 384, 384)],
                           occ[bz, bx, :, :, 256:512].reshape(384, 256), preferred_element_type=F32)
            total = term if total is None else total + term
        return total

    ints_copy.wait()
    for copy in sib_a0 + sib_b0:
        copy.wait_recv()
    hacc[:, 0:256] = part_a(zl)
    hacc[:, 256:512] = part_b(x)
    for copy in sib_a1 + sib_b1:
        copy.wait_recv()
    hacc[:, 0:256] += part_a(zd)
    hacc[:, 256:512] += part_b(xl)
    hacc[:, 0:256] += part_a(zr)
    hacc[:, 256:512] += part_b(xr)
    sib_2 = []
    for (t, u, bx), (v, w, bz) in zip(last_a, last_b):
        t.wait_recv()
        u.wait_recv()
        sib_2.append(same(blk(zo, bx, ALL, PA), sibling))
        v.wait_recv()
        w.wait_recv()
        sib_2.append(same(blk(bz, xo, ALL, PB), sibling))
    for copy in sib_2:
        copy.wait_recv()
    h_a = (hacc[:, 0:256] + part_a(zo)).astype(BF16)
    h_b = (hacc[:, 256:512] + part_b(xo)).astype(BF16)
    hrow[x, :, 0:256] = h_a
    hrow[x, :, 256:512] = h_b
    for s in range(3):
        hcol[s, zl, c, :, 0:256] = h_a[64 * s:64 * s + 64]
        hcol[s, zl, c, :, 256:512] = h_b[64 * s:64 * s + 64]

    r_e, r_w = same(hrow.at[x], east), same(hrow.at[x], west)
    c_in = []
    for s in range(3):
        c_in.append([same(hcol.at[s, zl, c], in_group(d)) for d in (1, 3, 2)])
    c_sib = [[same(hcol.at[s, zl, c], sibling)] for s in range(3)]
    r_e.wait_recv()
    r_et = same(hrow.at[xl, TOP], east)
    r_w.wait_recv()
    r_wb = same(hrow.at[xr, BOT], west)

    yr, yl, yo = up(y, 1), up(y, -1), up(y, 2)
    y_up, y_dn = at(dy=1), at(dy=-1)
    hr, hl, ho = up(zh, 1), up(zh, -1), up(zh, 2)
    z_up, z_dn = at(dz=4), at(dz=-4)
    A, B = pl.ds(0, 384), pl.ds(384, 384)
    TA, TB = pl.ds(0, 96), pl.ds(96, 96)
    y1, y2, xs, z1, z2 = {}, {}, {}, {}, {}

    def columns_in(s):
        for copy, d in zip(c_in[s], (3, 1, 2)):
            copy.wait_recv()
            c_sib[s].append(same(hcol.at[s, up(zl, d), c], sibling))
        for copy in c_sib[s]:
            copy.wait_recv()

    def product(s):
        for half in range(2):
            cols = hcol[s, 2 * half:2 * half + 2].reshape(256, 512)
            for bx in range(4):
                p = lax.dot_general(hrow[bx], cols, (((1,), (1,)), ((), ())), preferred_element_type=F32)
                p = p.astype(BF16)
                pb[s, 2 * half, 192 * bx:192 * bx + 192] = p[:, 0:128]
                pb[s, 2 * half + 1, 192 * bx:192 * bx + 192] = p[:, 128:256]

    def y_first(s):
        y1[s] = (send(pb.at[s, yo, A], yin.at[s, 0], y_up),
                 send(pb.at[s, yo, B], yin.at[s, 1], y_dn),
                 send(pb.at[s, yr, B], yin.at[s, 2], y_up),
                 send(pb.at[s, yl, A], yin.at[s, 3], y_dn))

    def y_second(s):
        y1[s][0].wait_recv()
        pb[s, yr, A] = (pb[s, yr, A].astype(F32) + yin[s, 0].astype(F32)).astype(BF16)
        up_copy = send(pb.at[s, yr, A], yin.at[s, 4], y_up)
        y1[s][1].wait_recv()
        pb[s, yl, B] = (pb[s, yl, B].astype(F32) + yin[s, 1].astype(F32)).astype(BF16)
        y2[s] = (up_copy, send(pb.at[s, yl, B], yin.at[s, 5], y_dn))

    def y_last(s):
        for copy in y1[s][2:] + y2[s]:
            copy.wait_recv()
        ysum[s, 0:2] = (pb[s, y, A].astype(F32) + yin[s, 3].astype(F32)
                        + yin[s, 4].astype(F32)).astype(BF16).reshape(2, 192, 128)
        ysum[s, 2:4] = (pb[s, y, B].astype(F32) + yin[s, 2].astype(F32)
                        + yin[s, 5].astype(F32)).astype(BF16).reshape(2, 192, 128)
        xs[s] = [send(ysum.at[s, up(x, d)], xin.at[s, x], at(dx=d)) for d in (2, 1, -1)]
        xin[s, x] = ysum[s, x]

    def z_first(s):
        for copy in xs[s]:
            copy.wait_recv()
        z1[s] = (send(xin.at[s, ho, TA], zin.at[s, 0], z_up),
                 send(xin.at[s, ho, TB], zin.at[s, 1], z_dn),
                 send(xin.at[s, hr, TB], zin.at[s, 2], z_up),
                 send(xin.at[s, hl, TA], zin.at[s, 3], z_dn))

    def z_second(s):
        z1[s][0].wait_recv()
        zbuf[s, 0] = (xin[s, hr, TA].astype(F32) + zin[s, 0].astype(F32)).astype(BF16)
        up_copy = send(zbuf.at[s, 0], zin.at[s, 4], z_up)
        z1[s][1].wait_recv()
        zbuf[s, 1] = (xin[s, hl, TB].astype(F32) + zin[s, 1].astype(F32)).astype(BF16)
        z2[s] = (up_copy, send(zbuf.at[s, 1], zin.at[s, 5], z_dn))

    def z_last(s):
        for copy in z1[s][2:] + z2[s]:
            copy.wait_recv()
        top = xin[s, zh, TA].astype(F32) + zin[s, 3].astype(F32) + zin[s, 4].astype(F32)
        bot = xin[s, zh, TB].astype(F32) + zin[s, 2].astype(F32) + zin[s, 5].astype(F32)
        for rows, v in ((slice(0, 96), top), (slice(96, 192), bot)):
            out_ref[rows, 64 * s:64 * s + 64] = v[:, 0:64]
            out_ref[rows, 192 + 64 * s:192 + 64 * s + 64] = v[:, 64:128]

    columns_in(0)
    r_et.wait_recv()
    r_wb.wait_recv()
    product(0)
    y_first(0)
    y_second(0)
    columns_in(1)
    product(1)
    y_first(1)
    y_last(0)
    y_second(1)
    columns_in(2)
    product(2)
    y_first(2)
    z_first(0)
    y_last(1)
    y_second(2)
    z_second(0)
    z_first(1)
    y_last(2)
    z_second(1)
    z_last(0)
    z_first(2)
    z_last(1)
    z_second(2)
    z_last(2)
    for copy in copies:
        copy.wait_send()


def local(integrals, occupied):
    return pl.pallas_call(
        kernel,
        out_shape=jax.ShapeDtypeStruct((192, 384), F32),
        in_specs=[pl.BlockSpec(memory_space=pl.ANY)] * 2,
        out_specs=pl.BlockSpec(memory_space=pltpu.VMEM),
        scratch_shapes=[
            pltpu.VMEM((4, 4, 2, 192, 512), BF16),
            pltpu.VMEM((192, 6144), BF16),
            pltpu.VMEM((192, 512), F32),
            pltpu.VMEM((4, 192, 512), BF16),
            pltpu.VMEM((3, 4, 2, 64, 512), BF16),
            pltpu.VMEM((3, 4, 768, 128), BF16),
            pltpu.VMEM((3, 6, 384, 128), BF16),
            pltpu.VMEM((3, 4, 192, 128), BF16),
            pltpu.VMEM((3, 4, 192, 128), BF16),
            pltpu.VMEM((3, 6, 96, 128), BF16),
            pltpu.VMEM((3, 2, 96, 128), BF16),
            pltpu.SemaphoreType.DMA((N_SEM,)),
            pltpu.SemaphoreType.DMA((N_SEM,)),
            pltpu.SemaphoreType.DMA((2,)),
        ],
        compiler_params=pltpu.CompilerParams(
            collective_id=0, has_side_effects=True, vmem_limit_bytes=60 << 20),
        name="exchange",
    )(integrals.reshape(192, 6144), occupied)


def solution(mesh):
    in_specs = (P("grp", "row", None), P("row", None))
    return jax.shard_map(local, mesh=mesh, in_specs=in_specs, out_specs=P("row", "grp"), check_vma=False)
```

```python
import jax
import jax.numpy as jnp
from jax import lax
from jax.experimental import pallas as pl
from jax.experimental.pallas import tpu as pltpu
from jax.sharding import PartitionSpec as P

MESH = pl.DeviceIdType.MESH
F32 = jnp.float32
BF16 = jnp.bfloat16

N_SEM = 192


def kernel(ints_hbm, occ_hbm, out_ref, occ, ints, hacc, hrow, hcol, pb,
           yin, ysum, xin, zin, zbuf, ssem, rsem, lsem):
    grp, row = lax.axis_index("grp"), lax.axis_index("row")
    y, zh = grp // 4, grp % 4
    zl, x, c = row // 8, (row // 2) % 4, row % 2
    z = zh * 4 + zl

    def up(v, d, n=4):
        return (v + d + n) % n

    def at(dx=0, dy=0, dz=0):
        zz = up(z, dz, 16)
        return (up(y, dy) * 4 + zz // 4, (zz % 4) * 8 + up(x, dx) * 2 + c)

    def in_group(d):
        return (grp, up(zl, d) * 8 + x * 2 + c)

    sibling = (grp, zl * 8 + x * 2 + (1 - c))

    copies = []

    def send(src, dst, to):
        k = len(copies)
        copy = pltpu.make_async_remote_copy(
            src_ref=src, dst_ref=dst, send_sem=ssem.at[k], recv_sem=rsem.at[k],
            device_id=to, device_id_type=MESH)
        copy.start()
        copies.append(copy)
        return copy

    def same(ref, to):
        return send(ref, ref, to)

    own_copy = pltpu.make_async_copy(occ_hbm, occ.at[zl, x, c], lsem.at[0])
    own_copy.start()
    ints_copy = pltpu.make_async_copy(ints_hbm, ints, lsem.at[1])
    ints_copy.start()

    barrier = pltpu.get_barrier_semaphore()
    partners = [sibling, at(dx=1), at(dx=2), at(dx=-1), at(dy=1), at(dy=-1), at(dz=1), at(dz=-1),
                at(dz=4), at(dz=-4), in_group(1), in_group(2), in_group(3)]
    for partner in partners:
        pl.semaphore_signal(barrier, inc=1, device_id=partner, device_id_type=MESH)
    pl.semaphore_wait(barrier, len(partners))
    own_copy.wait()

    xr, xl, xo = up(x, 1), up(x, -1), up(x, 2)
    zr, zd, zo = up(zl, 1), up(zl, -1), up(zl, 2)
    east, west, north, south = at(dx=1), at(dx=-1), at(dz=1), at(dz=-1)
    PA, PB = pl.ds(0, 256), pl.ds(256, 256)
    ALL, TOP, BOT = pl.ds(0, 192), pl.ds(0, 96), pl.ds(96, 96)

    def blk(bz, bx, rows, cols):
        return occ.at[bz, bx, c, rows, cols]

    fwd_a = [[], []]
    fwd_b = [[], []]
    own_a, own_b = blk(zl, x, ALL, PA), blk(zl, x, ALL, PB)
    a_e, a_w = same(own_a, east), same(own_a, west)
    b_n, b_s = same(own_b, north), same(own_b, south)
    fwd_a[0].append(same(own_a, north))
    fwd_a[1].append(same(own_a, south))
    fwd_b[0].append(same(own_b, east))
    fwd_b[1].append(same(own_b, west))
    sib_own = same(occ.at[zl, x, c], sibling)

    a_e.wait_recv()
    a_et = same(blk(zl, xl, TOP, PA), east)
    fwd_a[0].append(same(blk(zl, xl, ALL, PA), north))
    fwd_a[1].append(same(blk(zl, xl, ALL, PA), south))
    b_n.wait_recv()
    b_nt = same(blk(zd, x, TOP, PB), north)
    fwd_b[0].append(same(blk(zd, x, ALL, PB), east))
    fwd_b[1].append(same(blk(zd, x, ALL, PB), west))
    a_w.wait_recv()
    a_wb = same(blk(zl, xr, BOT, PA), west)
    fwd_a[0].append(same(blk(zl, xr, ALL, PA), north))
    fwd_a[1].append(same(blk(zl, xr, ALL, PA), south))
    b_s.wait_recv()
    b_sb = same(blk(zr, x, BOT, PB), south)
    fwd_b[0].append(same(blk(zr, x, ALL, PB), east))
    fwd_b[1].append(same(blk(zr, x, ALL, PB), west))
    sib_a0 = [sib_own, same(blk(zl, xl, ALL, PA), sibling), same(blk(zl, xr, ALL, PA), sibling)]
    sib_b0 = [same(blk(zd, x, ALL, PB), sibling), same(blk(zr, x, ALL, PB), sibling)]
    a_et.wait_recv()
    a_wb.wait_recv()
    fwd_a[0].append(same(blk(zl, xo, ALL, PA), north))
    fwd_a[1].append(same(blk(zl, xo, ALL, PA), south))
    sib_a0.append(same(blk(zl, xo, ALL, PA), sibling))
    b_nt.wait_recv()
    b_sb.wait_recv()
    fwd_b[0].append(same(blk(zo, x, ALL, PB), east))
    fwd_b[1].append(same(blk(zo, x, ALL, PB), west))
    sib_b0.append(same(blk(zo, x, ALL, PB), sibling))

    last_a, last_b = [], []
    sib_a1, sib_b1 = [], []
    for bx, bz, j in zip((x, xl, xr, xo), (zl, zd, zr, zo), range(4)):
        fwd_a[0][j].wait_recv()
        t = same(blk(zd, bx, TOP, PA), north)
        sib_a1.append(same(blk(zd, bx, ALL, PA), sibling))
        fwd_a[1][j].wait_recv()
        u = same(blk(zr, bx, BOT, PA), south)
        sib_a1.append(same(blk(zr, bx, ALL, PA), sibling))
        last_a.append((t, u, bx))
        fwd_b[0][j].wait_recv()
        t = same(blk(bz, xl, TOP, PB), east)
        sib_b1.append(same(blk(bz, xl, ALL, PB), sibling))
        fwd_b[1][j].wait_recv()
        u = same(blk(bz, xr, BOT, PB), west)
        sib_b1.append(same(blk(bz, xr, ALL, PB), sibling))
        last_b.append((t, u, bz))

    def lanes(start, size):
        return pl.ds(pl.multiple_of(start, 128), size)

    def part_a(bz):
        return jnp.dot(ints[:, lanes(bz * 1536, 1536)],
                       occ[bz, :, :, :, 0:256].reshape(1536, 256), preferred_element_type=F32)

    def part_b(bx):
        total = None
        for bz in range(4):
            term = jnp.dot(ints[:, lanes(bz * 1536 + bx * 384, 384)],
                           occ[bz, bx, :, :, 256:512].reshape(384, 256), preferred_element_type=F32)
            total = term if total is None else total + term
        return total

    ints_copy.wait()
    for copy in sib_a0 + sib_b0:
        copy.wait_recv()
    hacc[:, 0:256] = part_a(zl)
    hacc[:, 256:512] = part_b(x)
    for copy in sib_a1 + sib_b1:
        copy.wait_recv()
    hacc[:, 0:256] += part_a(zd)
    hacc[:, 256:512] += part_b(xl)
    hacc[:, 0:256] += part_a(zr)
    hacc[:, 256:512] += part_b(xr)
    sib_2 = []
    for (t, u, bx), (v, w, bz) in zip(last_a, last_b):
        t.wait_recv()
        u.wait_recv()
        sib_2.append(same(blk(zo, bx, ALL, PA), sibling))
        v.wait_recv()
        w.wait_recv()
        sib_2.append(same(blk(bz, xo, ALL, PB), sibling))
    for copy in sib_2:
        copy.wait_recv()
    h_a = (hacc[:, 0:256] + part_a(zo)).astype(BF16)
    h_b = (hacc[:, 256:512] + part_b(xo)).astype(BF16)
    hrow[x, :, 0:256] = h_a
    hrow[x, :, 256:512] = h_b
    for s in range(3):
        hcol[s, zl, c, :, 0:256] = h_a[64 * s:64 * s + 64]
        hcol[s, zl, c, :, 256:512] = h_b[64 * s:64 * s + 64]

    def columns_out(s):
        return [same(hcol.at[s, zl, c], in_group(d)) for d in (1, 3, 2)]

    r_e, r_w = same(hrow.at[x, TOP], east), same(hrow.at[x, BOT], west)
    c_in = [columns_out(0)]
    r_e2, r_w2 = same(hrow.at[x, BOT], east), same(hrow.at[x, TOP], west)
    c_in += [columns_out(1), columns_out(2)]
    c_sib = [[same(hcol.at[s, zl, c], sibling)] for s in range(3)]
    r_e.wait_recv()
    r_et = same(hrow.at[xl, TOP], east)
    r_w.wait_recv()
    r_wb = same(hrow.at[xr, BOT], west)

    yr, yl, yo = up(y, 1), up(y, -1), up(y, 2)
    y_up, y_dn = at(dy=1), at(dy=-1)
    hr, hl, ho = up(zh, 1), up(zh, -1), up(zh, 2)
    z_up, z_dn = at(dz=4), at(dz=-4)
    A, B = pl.ds(0, 192), pl.ds(192, 192)
    TA, TB = pl.ds(0, 48), pl.ds(48, 48)
    y1, y2, xs, z1, z2 = {}, {}, {}, {}, {}

    def columns_in(s):
        for copy, d in zip(c_in[s], (3, 1, 2)):
            copy.wait_recv()
            c_sib[s].append(same(hcol.at[s, up(zl, d), c], sibling))
        for copy in c_sib[s]:
            copy.wait_recv()

    def product(s):
        for half in range(2):
            cols = hcol[s, 2 * half:2 * half + 2].reshape(256, 512)
            for bx in range(4):
                p = lax.dot_general(hrow[bx], cols, (((1,), (1,)), ((), ())), preferred_element_type=F32)
                p = p.astype(BF16)
                for t in range(2):
                    for j in range(2):
                        pb[2 * s + t, 2 * half + j, 96 * bx:96 * bx + 96] = (
                            p[96 * t:96 * t + 96, 128 * j:128 * j + 128])

    def y_first(k):
        if k % 2 == 0:
            columns_in(k // 2)
            if k == 0:
                for copy in (r_e2, r_w2, r_et, r_wb):
                    copy.wait_recv()
            product(k // 2)
        y1[k] = (send(pb.at[k, yo, A], yin.at[k, 0], y_up),
                 send(pb.at[k, yo, B], yin.at[k, 1], y_dn),
                 send(pb.at[k, yr, B], yin.at[k, 2], y_up),
                 send(pb.at[k, yl, A], yin.at[k, 3], y_dn))

    def y_second(k):
        y1[k][0].wait_recv()
        pb[k, yr, A] = (pb[k, yr, A].astype(F32) + yin[k, 0].astype(F32)).astype(BF16)
        up_copy = send(pb.at[k, yr, A], yin.at[k, 4], y_up)
        y1[k][1].wait_recv()
        pb[k, yl, B] = (pb[k, yl, B].astype(F32) + yin[k, 1].astype(F32)).astype(BF16)
        y2[k] = (up_copy, send(pb.at[k, yl, B], yin.at[k, 5], y_dn))

    def y_last(k):
        for copy in y1[k][2:] + y2[k]:
            copy.wait_recv()
        ysum[k, 0:2] = (pb[k, y, A].astype(F32) + yin[k, 3].astype(F32)
                        + yin[k, 4].astype(F32)).astype(BF16).reshape(2, 96, 128)
        ysum[k, 2:4] = (pb[k, y, B].astype(F32) + yin[k, 2].astype(F32)
                        + yin[k, 5].astype(F32)).astype(BF16).reshape(2, 96, 128)
        xs[k] = [send(ysum.at[k, up(x, d)], xin.at[k, x], at(dx=d)) for d in (2, 1, -1)]
        xin[k, x] = ysum[k, x]

    def z_first(k):
        for copy in xs[k]:
            copy.wait_recv()
        z1[k] = (send(xin.at[k, ho, TA], zin.at[k, 0], z_up),
                 send(xin.at[k, ho, TB], zin.at[k, 1], z_dn),
                 send(xin.at[k, hr, TB], zin.at[k, 2], z_up),
                 send(xin.at[k, hl, TA], zin.at[k, 3], z_dn))

    def z_second(k):
        z1[k][0].wait_recv()
        zbuf[k, 0] = (xin[k, hr, TA].astype(F32) + zin[k, 0].astype(F32)).astype(BF16)
        up_copy = send(zbuf.at[k, 0], zin.at[k, 4], z_up)
        z1[k][1].wait_recv()
        zbuf[k, 1] = (xin[k, hl, TB].astype(F32) + zin[k, 1].astype(F32)).astype(BF16)
        z2[k] = (up_copy, send(zbuf.at[k, 1], zin.at[k, 5], z_dn))

    def z_last(k):
        for copy in z1[k][2:] + z2[k]:
            copy.wait_recv()
        top = xin[k, zh, TA].astype(F32) + zin[k, 3].astype(F32) + zin[k, 4].astype(F32)
        bot = xin[k, zh, TB].astype(F32) + zin[k, 2].astype(F32) + zin[k, 5].astype(F32)
        s, t = k // 2, k % 2
        for first, v in ((96 * t, top), (96 * t + 48, bot)):
            out_ref[first:first + 48, 64 * s:64 * s + 64] = v[:, 0:64]
            out_ref[first:first + 48, 192 + 64 * s:192 + 64 * s + 64] = v[:, 64:128]

    steps = ((z_last, 7), (z_second, 5), (z_first, 3), (y_last, 2), (y_second, 1), (y_first, 0))
    for i in range(6 + 7):
        for step, lag in steps:
            if 0 <= i - lag < 6:
                step(i - lag)
    for copy in copies:
        copy.wait_send()


def local(integrals, occupied):
    return pl.pallas_call(
        kernel,
        out_shape=jax.ShapeDtypeStruct((192, 384), F32),
        in_specs=[pl.BlockSpec(memory_space=pltpu.HBM)] * 2,
        out_specs=pl.BlockSpec(memory_space=pltpu.VMEM),
        scratch_shapes=[
            pltpu.VMEM((4, 4, 2, 192, 512), BF16),
            pltpu.VMEM((192, 6144), BF16),
            pltpu.VMEM((192, 512), F32),
            pltpu.VMEM((4, 192, 512), BF16),
            pltpu.VMEM((3, 4, 2, 64, 512), BF16),
            pltpu.VMEM((6, 4, 384, 128), BF16),
            pltpu.VMEM((6, 6, 192, 128), BF16),
            pltpu.VMEM((6, 4, 96, 128), BF16),
            pltpu.VMEM((6, 4, 96, 128), BF16),
            pltpu.VMEM((6, 6, 48, 128), BF16),
            pltpu.VMEM((6, 2, 48, 128), BF16),
            pltpu.SemaphoreType.DMA((N_SEM,)),
            pltpu.SemaphoreType.DMA((N_SEM,)),
            pltpu.SemaphoreType.DMA((2,)),
        ],
        compiler_params=pltpu.CompilerParams(
            collective_id=0, has_side_effects=True, vmem_limit_bytes=48 << 20),
        name="exchange",
    )(integrals.reshape(192, 6144), occupied)


def solution(mesh):
    in_specs = (P("grp", "row", None), P("row", None))
    return jax.shard_map(local, mesh=mesh, in_specs=in_specs, out_specs=P("row", "grp"), check_vma=False)
```

```python
import jax
import jax.numpy as jnp
from jax import lax
from jax.experimental import pallas as pl
from jax.experimental.pallas import tpu as pltpu
from jax.sharding import PartitionSpec as P

MESH = pl.DeviceIdType.MESH
F32 = jnp.float32
BF16 = jnp.bfloat16

N_SEM = 192


def kernel(ints_hbm, occ_hbm, out_ref, occ, ints, hacc, hrow, hcol, pb,
           yin, ysum, xin, zin, zbuf, ssem, rsem, lsem):
    grp, row = lax.axis_index("grp"), lax.axis_index("row")
    y, zh = grp // 4, grp % 4
    zl, x, c = row // 8, (row // 2) % 4, row % 2
    z = zh * 4 + zl

    def up(v, d, n=4):
        return (v + d + n) % n

    def at(dx=0, dy=0, dz=0):
        zz = up(z, dz, 16)
        return (up(y, dy) * 4 + zz // 4, (zz % 4) * 8 + up(x, dx) * 2 + c)

    def in_group(d):
        return (grp, up(zl, d) * 8 + x * 2 + c)

    sibling = (grp, zl * 8 + x * 2 + (1 - c))

    copies = []

    def send(src, dst, to):
        k = len(copies)
        copy = pltpu.make_async_remote_copy(
            src_ref=src, dst_ref=dst, send_sem=ssem.at[k], recv_sem=rsem.at[k],
            device_id=to, device_id_type=MESH)
        copy.start()
        copies.append(copy)
        return copy

    def same(ref, to):
        return send(ref, ref, to)

    own_copy = pltpu.make_async_copy(occ_hbm, occ.at[zl, x, c], lsem.at[0])
    own_copy.start()
    ints_copy = pltpu.make_async_copy(ints_hbm, ints, lsem.at[1])
    ints_copy.start()

    barrier = pltpu.get_barrier_semaphore()
    partners = [sibling, at(dx=1), at(dx=2), at(dx=-1), at(dy=1), at(dy=-1), at(dz=1), at(dz=-1),
                at(dz=4), at(dz=-4), in_group(1), in_group(2), in_group(3)]
    for partner in partners:
        pl.semaphore_signal(barrier, inc=1, device_id=partner, device_id_type=MESH)
    pl.semaphore_wait(barrier, len(partners))
    own_copy.wait()

    xr, xl, xo = up(x, 1), up(x, -1), up(x, 2)
    zr, zd, zo = up(zl, 1), up(zl, -1), up(zl, 2)
    east, west, north, south = at(dx=1), at(dx=-1), at(dz=1), at(dz=-1)
    PA, PB = pl.ds(0, 256), pl.ds(256, 256)
    ALL, TOP, BOT = pl.ds(0, 192), pl.ds(0, 96), pl.ds(96, 96)

    def blk(bz, bx, rows, cols):
        return occ.at[bz, bx, c, rows, cols]

    fwd_a = [[], []]
    fwd_b = [[], []]
    own_a, own_b = blk(zl, x, ALL, PA), blk(zl, x, ALL, PB)
    a_e, a_w = same(own_a, east), same(own_a, west)
    b_n, b_s = same(own_b, north), same(own_b, south)
    fwd_a[0].append(same(own_a, north))
    fwd_a[1].append(same(own_a, south))
    fwd_b[0].append(same(own_b, east))
    fwd_b[1].append(same(own_b, west))
    sib_own = same(occ.at[zl, x, c], sibling)

    a_e.wait_recv()
    a_et = same(blk(zl, xl, TOP, PA), east)
    fwd_a[0].append(same(blk(zl, xl, ALL, PA), north))
    fwd_a[1].append(same(blk(zl, xl, ALL, PA), south))
    b_n.wait_recv()
    b_nt = same(blk(zd, x, TOP, PB), north)
    fwd_b[0].append(same(blk(zd, x, ALL, PB), east))
    fwd_b[1].append(same(blk(zd, x, ALL, PB), west))
    a_w.wait_recv()
    a_wb = same(blk(zl, xr, BOT, PA), west)
    fwd_a[0].append(same(blk(zl, xr, ALL, PA), north))
    fwd_a[1].append(same(blk(zl, xr, ALL, PA), south))
    b_s.wait_recv()
    b_sb = same(blk(zr, x, BOT, PB), south)
    fwd_b[0].append(same(blk(zr, x, ALL, PB), east))
    fwd_b[1].append(same(blk(zr, x, ALL, PB), west))
    sib_a0 = [sib_own, same(blk(zl, xl, ALL, PA), sibling), same(blk(zl, xr, ALL, PA), sibling)]
    sib_b0 = [same(blk(zd, x, ALL, PB), sibling), same(blk(zr, x, ALL, PB), sibling)]
    a_et.wait_recv()
    a_wb.wait_recv()
    fwd_a[0].append(same(blk(zl, xo, ALL, PA), north))
    fwd_a[1].append(same(blk(zl, xo, ALL, PA), south))
    sib_a0.append(same(blk(zl, xo, ALL, PA), sibling))
    b_nt.wait_recv()
    b_sb.wait_recv()
    fwd_b[0].append(same(blk(zo, x, ALL, PB), east))
    fwd_b[1].append(same(blk(zo, x, ALL, PB), west))
    sib_b0.append(same(blk(zo, x, ALL, PB), sibling))

    last_a, last_b = [], []
    sib_a1, sib_b1 = [], []
    for bx, bz, j in zip((x, xl, xr, xo), (zl, zd, zr, zo), range(4)):
        fwd_a[0][j].wait_recv()
        t = same(blk(zd, bx, TOP, PA), north)
        sib_a1.append(same(blk(zd, bx, ALL, PA), sibling))
        fwd_a[1][j].wait_recv()
        u = same(blk(zr, bx, BOT, PA), south)
        sib_a1.append(same(blk(zr, bx, ALL, PA), sibling))
        last_a.append((t, u, bx))
        fwd_b[0][j].wait_recv()
        t = same(blk(bz, xl, TOP, PB), east)
        sib_b1.append(same(blk(bz, xl, ALL, PB), sibling))
        fwd_b[1][j].wait_recv()
        u = same(blk(bz, xr, BOT, PB), west)
        sib_b1.append(same(blk(bz, xr, ALL, PB), sibling))
        last_b.append((t, u, bz))

    def lanes(start, size):
        return pl.ds(pl.multiple_of(start, 128), size)

    def part_a(bz):
        return jnp.dot(ints[:, lanes(bz * 1536, 1536)],
                       occ[bz, :, :, :, 0:256].reshape(1536, 256), preferred_element_type=F32)

    def part_b(bx):
        total = None
        for bz in range(4):
            term = jnp.dot(ints[:, lanes(bz * 1536 + bx * 384, 384)],
                           occ[bz, bx, :, :, 256:512].reshape(384, 256), preferred_element_type=F32)
            total = term if total is None else total + term
        return total

    ints_copy.wait()
    for copy in sib_a0 + sib_b0:
        copy.wait_recv()
    hacc[:, 0:256] = part_a(zl)
    hacc[:, 256:512] = part_b(x)
    for copy in sib_a1 + sib_b1:
        copy.wait_recv()
    hacc[:, 0:256] += part_a(zd)
    hacc[:, 256:512] += part_b(xl)
    hacc[:, 0:256] += part_a(zr)
    hacc[:, 256:512] += part_b(xr)
    sib_2 = []
    for (t, u, bx), (v, w, bz) in zip(last_a, last_b):
        t.wait_recv()
        u.wait_recv()
        sib_2.append(same(blk(zo, bx, ALL, PA), sibling))
        v.wait_recv()
        w.wait_recv()
        sib_2.append(same(blk(bz, xo, ALL, PB), sibling))
    for copy in sib_2:
        copy.wait_recv()
    h_a = (hacc[:, 0:256] + part_a(zo)).astype(BF16)
    h_b = (hacc[:, 256:512] + part_b(xo)).astype(BF16)
    hrow[x, :, 0:256] = h_a
    hrow[x, :, 256:512] = h_b
    for s in range(3):
        hcol[s, zl, c, :, 0:256] = h_a[64 * s:64 * s + 64]
        hcol[s, zl, c, :, 256:512] = h_b[64 * s:64 * s + 64]

    def columns_out(s):
        return [same(hcol.at[s, zl, c], in_group(d)) for d in (1, 3, 2)]

    Q = [pl.ds(48 * j, 48) for j in range(4)]
    r_in = [[same(hrow.at[x, TOP], east), same(hrow.at[x, TOP], west)]]
    c_in = [columns_out(0)]
    r_in.append([same(hrow.at[x, BOT], east), same(hrow.at[x, BOT], west)])
    c_in += [columns_out(1), columns_out(2)]
    c_sib = [[same(hcol.at[s, zl, c], sibling)] for s in range(3)]
    for t in range(2):
        for copy in r_in[t]:
            copy.wait_recv()
        r_in[t] = [same(hrow.at[xl, Q[2 * t]], east), same(hrow.at[xr, Q[2 * t + 1]], west)]

    yr, yl, yo = up(y, 1), up(y, -1), up(y, 2)
    y_up, y_dn = at(dy=1), at(dy=-1)
    hr, hl, ho = up(zh, 1), up(zh, -1), up(zh, 2)
    z_up, z_dn = at(dz=4), at(dz=-4)
    A, B = pl.ds(0, 192), pl.ds(192, 192)
    TA, TB = pl.ds(0, 48), pl.ds(48, 48)
    y1, y2, xs, z1, z2 = {}, {}, {}, {}, {}

    def columns_in(s):
        for copy, d in zip(c_in[s], (3, 1, 2)):
            copy.wait_recv()
            c_sib[s].append(same(hcol.at[s, up(zl, d), c], sibling))
        for copy in c_sib[s]:
            copy.wait_recv()

    def product(k):
        s, t = k // 2, k % 2
        rows = hrow[:, 96 * t:96 * t + 96].reshape(384, 512)
        for half in range(2):
            cols = hcol[s, 2 * half:2 * half + 2].reshape(256, 512)
            p = lax.dot_general(rows, cols, (((1,), (1,)), ((), ())), preferred_element_type=F32)
            p = p.astype(BF16)
            pb[k, 2 * half] = p[:, 0:128]
            pb[k, 2 * half + 1] = p[:, 128:256]

    def y_first(k):
        if k % 2 == 0:
            columns_in(k // 2)
        if k < 2:
            for copy in r_in[k]:
                copy.wait_recv()
        product(k)
        y1[k] = (send(pb.at[k, yo, A], yin.at[k, 0], y_up),
                 send(pb.at[k, yo, B], yin.at[k, 1], y_dn),
                 send(pb.at[k, yr, B], yin.at[k, 2], y_up),
                 send(pb.at[k, yl, A], yin.at[k, 3], y_dn))

    def y_second(k):
        y1[k][0].wait_recv()
        pb[k, yr, A] = (pb[k, yr, A].astype(F32) + yin[k, 0].astype(F32)).astype(BF16)
        up_copy = send(pb.at[k, yr, A], yin.at[k, 4], y_up)
        y1[k][1].wait_recv()
        pb[k, yl, B] = (pb[k, yl, B].astype(F32) + yin[k, 1].astype(F32)).astype(BF16)
        y2[k] = (up_copy, send(pb.at[k, yl, B], yin.at[k, 5], y_dn))

    def y_last(k):
        for copy in y1[k][2:] + y2[k]:
            copy.wait_recv()
        ysum[k, 0:2] = (pb[k, y, A].astype(F32) + yin[k, 3].astype(F32)
                        + yin[k, 4].astype(F32)).astype(BF16).reshape(2, 96, 128)
        ysum[k, 2:4] = (pb[k, y, B].astype(F32) + yin[k, 2].astype(F32)
                        + yin[k, 5].astype(F32)).astype(BF16).reshape(2, 96, 128)
        xs[k] = [send(ysum.at[k, up(x, d)], xin.at[k, x], at(dx=d)) for d in (2, 1, -1)]
        xin[k, x] = ysum[k, x]

    def z_first(k):
        for copy in xs[k]:
            copy.wait_recv()
        z1[k] = (send(xin.at[k, ho, TA], zin.at[k, 0], z_up),
                 send(xin.at[k, ho, TB], zin.at[k, 1], z_dn),
                 send(xin.at[k, hr, TB], zin.at[k, 2], z_up),
                 send(xin.at[k, hl, TA], zin.at[k, 3], z_dn))

    def z_second(k):
        z1[k][0].wait_recv()
        zbuf[k, 0] = (xin[k, hr, TA].astype(F32) + zin[k, 0].astype(F32)).astype(BF16)
        up_copy = send(zbuf.at[k, 0], zin.at[k, 4], z_up)
        z1[k][1].wait_recv()
        zbuf[k, 1] = (xin[k, hl, TB].astype(F32) + zin[k, 1].astype(F32)).astype(BF16)
        z2[k] = (up_copy, send(zbuf.at[k, 1], zin.at[k, 5], z_dn))

    def z_last(k):
        for copy in z1[k][2:] + z2[k]:
            copy.wait_recv()
        top = xin[k, zh, TA].astype(F32) + zin[k, 3].astype(F32) + zin[k, 4].astype(F32)
        bot = xin[k, zh, TB].astype(F32) + zin[k, 2].astype(F32) + zin[k, 5].astype(F32)
        s, t = k // 2, k % 2
        for first, v in ((96 * t, top), (96 * t + 48, bot)):
            out_ref[first:first + 48, 64 * s:64 * s + 64] = v[:, 0:64]
            out_ref[first:first + 48, 192 + 64 * s:192 + 64 * s + 64] = v[:, 64:128]

    steps = {"F": y_first, "S": y_second, "L": y_last, "f": z_first, "s": z_second, "l": z_last}
    for part in ("F0F1S0F2S1F3L0S2F4", "L1S3F5f0L2f1S4L3S5f2s0L4s1f3L5",
                 "s2l0f4f5s3l1s4l2s5l3l4l5"):
        for j in range(0, len(part), 2):
            steps[part[j]](int(part[j + 1]))
    for copy in copies:
        copy.wait_send()


def local(integrals, occupied):
    return pl.pallas_call(
        kernel,
        out_shape=jax.ShapeDtypeStruct((192, 384), F32),
        in_specs=[pl.BlockSpec(memory_space=pltpu.HBM)] * 2,
        out_specs=pl.BlockSpec(memory_space=pltpu.VMEM),
        scratch_shapes=[
            pltpu.VMEM((4, 4, 2, 192, 512), BF16),
            pltpu.VMEM((192, 6144), BF16),
            pltpu.VMEM((192, 512), F32),
            pltpu.VMEM((4, 192, 512), BF16),
            pltpu.VMEM((3, 4, 2, 64, 512), BF16),
            pltpu.VMEM((6, 4, 384, 128), BF16),
            pltpu.VMEM((6, 6, 192, 128), BF16),
            pltpu.VMEM((6, 4, 96, 128), BF16),
            pltpu.VMEM((6, 4, 96, 128), BF16),
            pltpu.VMEM((6, 6, 48, 128), BF16),
            pltpu.VMEM((6, 2, 48, 128), BF16),
            pltpu.SemaphoreType.DMA((N_SEM,)),
            pltpu.SemaphoreType.DMA((N_SEM,)),
            pltpu.SemaphoreType.DMA((2,)),
        ],
        compiler_params=pltpu.CompilerParams(
            collective_id=0, has_side_effects=True, vmem_limit_bytes=60 << 20),
        name="exchange",
    )(integrals.reshape(192, 6144), occupied)


def solution(mesh):
    in_specs = (P("grp", "row", None), P("row", None))
    return jax.shard_map(local, mesh=mesh, in_specs=in_specs, out_specs=P("row", "grp"), check_vma=False)
```

```python
import jax
import jax.numpy as jnp
from jax import lax
from jax.experimental import pallas as pl
from jax.experimental.pallas import tpu as pltpu
from jax.sharding import PartitionSpec as P

MESH = pl.DeviceIdType.MESH
F32 = jnp.float32
BF16 = jnp.bfloat16

N_SEM = 288


def kernel(ints_hbm, occ_hbm, out_ref, occ, ints, hacc, hrow, hcol, pb,
           yin, ysum, xin, zin, zbuf, ssem, rsem, lsem):
    grp, row = lax.axis_index("grp"), lax.axis_index("row")
    y, zh = grp // 4, grp % 4
    zl, x, c = row // 8, (row // 2) % 4, row % 2
    z = zh * 4 + zl

    def up(v, d, n=4):
        return (v + d + n) % n

    def at(dx=0, dy=0, dz=0):
        zz = up(z, dz, 16)
        return (up(y, dy) * 4 + zz // 4, (zz % 4) * 8 + up(x, dx) * 2 + c)

    def in_group(d):
        return (grp, up(zl, d) * 8 + x * 2 + c)

    sibling = (grp, zl * 8 + x * 2 + (1 - c))

    copies = []

    def send(src, dst, to):
        k = len(copies)
        copy = pltpu.make_async_remote_copy(
            src_ref=src, dst_ref=dst, send_sem=ssem.at[k], recv_sem=rsem.at[k],
            device_id=to, device_id_type=MESH)
        copy.start()
        copies.append(copy)
        return copy

    def same(ref, to):
        return send(ref, ref, to)

    own_copy = pltpu.make_async_copy(occ_hbm, occ.at[zl, x, c], lsem.at[0])
    own_copy.start()
    ints_copy = pltpu.make_async_copy(ints_hbm, ints, lsem.at[1])
    ints_copy.start()

    barrier = pltpu.get_barrier_semaphore()
    partners = [sibling, at(dx=1), at(dx=2), at(dx=-1), at(dy=1), at(dy=-1), at(dz=1), at(dz=-1),
                at(dz=4), at(dz=-4), in_group(1), in_group(2), in_group(3)]
    for partner in partners:
        pl.semaphore_signal(barrier, inc=1, device_id=partner, device_id_type=MESH)
    pl.semaphore_wait(barrier, len(partners))
    own_copy.wait()

    xr, xl, xo = up(x, 1), up(x, -1), up(x, 2)
    zr, zd, zo = up(zl, 1), up(zl, -1), up(zl, 2)
    east, west, north, south = at(dx=1), at(dx=-1), at(dz=1), at(dz=-1)
    y_up, y_dn = at(dy=1), at(dy=-1)
    PA, PB = pl.ds(0, 256), pl.ds(256, 256)
    odd = y % 2

    def rows_at(first, step, size):
        return pl.ds(pl.multiple_of(first + step * odd, 32), size)

    GOT, TOP, BOT = rows_at(0, 64, 128), rows_at(0, 64, 64), rows_at(64, 64, 64)
    UP, DOWN, LACK = rows_at(0, 160, 32), rows_at(32, 96, 32), rows_at(128, -128, 64)

    def blk(bz, bx, rows, cols):
        return occ.at[bz, bx, c, rows, cols]

    def over_y(bz, bx, cols):
        return [same(blk(bz, bx, UP, cols), y_up), same(blk(bz, bx, DOWN, cols), y_dn)]

    def landed(group):
        for copy in group:
            copy.wait_recv()

    fwd_a = [[], []]
    fwd_b = [[], []]
    own_a, own_b = blk(zl, x, GOT, PA), blk(zl, x, GOT, PB)
    a_e, a_w = same(own_a, east), same(own_a, west)
    b_n, b_s = same(own_b, north), same(own_b, south)
    fwd_a[0].append(same(own_a, north))
    fwd_a[1].append(same(own_a, south))
    fwd_b[0].append(same(own_b, east))
    fwd_b[1].append(same(own_b, west))
    sib_own = same(occ.at[zl, x, c], sibling)

    a_e.wait_recv()
    a_et = same(blk(zl, xl, TOP, PA), east)
    fwd_a[0].append(same(blk(zl, xl, GOT, PA), north))
    fwd_a[1].append(same(blk(zl, xl, GOT, PA), south))
    b_n.wait_recv()
    b_nt = same(blk(zd, x, TOP, PB), north)
    fwd_b[0].append(same(blk(zd, x, GOT, PB), east))
    fwd_b[1].append(same(blk(zd, x, GOT, PB), west))
    y_a0, y_b0 = [over_y(zl, xl, PA)], [over_y(zd, x, PB)]
    a_w.wait_recv()
    a_wb = same(blk(zl, xr, BOT, PA), west)
    fwd_a[0].append(same(blk(zl, xr, GOT, PA), north))
    fwd_a[1].append(same(blk(zl, xr, GOT, PA), south))
    b_s.wait_recv()
    b_sb = same(blk(zr, x, BOT, PB), south)
    fwd_b[0].append(same(blk(zr, x, GOT, PB), east))
    fwd_b[1].append(same(blk(zr, x, GOT, PB), west))
    y_a0.append(over_y(zl, xr, PA))
    y_b0.append(over_y(zr, x, PB))
    sib_0 = [sib_own, same(blk(zl, xl, GOT, PA), sibling), same(blk(zl, xr, GOT, PA), sibling),
             same(blk(zd, x, GOT, PB), sibling), same(blk(zr, x, GOT, PB), sibling)]
    landed((a_et, a_wb))
    fwd_a[0].append(same(blk(zl, xo, GOT, PA), north))
    fwd_a[1].append(same(blk(zl, xo, GOT, PA), south))
    y_a0.append(over_y(zl, xo, PA))
    landed((b_nt, b_sb))
    fwd_b[0].append(same(blk(zo, x, GOT, PB), east))
    fwd_b[1].append(same(blk(zo, x, GOT, PB), west))
    y_b0.append(over_y(zo, x, PB))
    sib_0 += [same(blk(zl, xo, GOT, PA), sibling), same(blk(zo, x, GOT, PB), sibling)]

    last = []
    sib_1 = []
    y_1 = [[], [], [], []]
    for bx, bz, j in zip((x, xl, xr, xo), (zl, zd, zr, zo), range(4)):
        fwd_a[0][j].wait_recv()
        t = same(blk(zd, bx, TOP, PA), north)
        fwd_a[1][j].wait_recv()
        u = same(blk(zr, bx, BOT, PA), south)
        fwd_b[0][j].wait_recv()
        v = same(blk(bz, xl, TOP, PB), east)
        fwd_b[1][j].wait_recv()
        w = same(blk(bz, xr, BOT, PB), west)
        last.append((t, u, v, w))
        y_1[0] += over_y(zd, bx, PA)
        y_1[1] += over_y(zr, bx, PA)
        y_1[2] += over_y(bz, xl, PB)
        y_1[3] += over_y(bz, xr, PB)
        sib_1 += [same(blk(zd, bx, GOT, PA), sibling), same(blk(zr, bx, GOT, PA), sibling),
                  same(blk(bz, xl, GOT, PB), sibling), same(blk(bz, xr, GOT, PB), sibling)]

    def lanes(start, size):
        return pl.ds(pl.multiple_of(start, 128), size)

    def part_a(bz):
        return jnp.dot(ints[:, lanes(bz * 1536, 1536)],
                       occ[bz, :, :, :, 0:256].reshape(1536, 256), preferred_element_type=F32)

    def part_b(bx):
        total = None
        for bz in range(4):
            term = jnp.dot(ints[:, lanes(bz * 1536 + bx * 384, 384)],
                           occ[bz, bx, :, :, 256:512].reshape(384, 256), preferred_element_type=F32)
            total = term if total is None else total + term
        return total

    def final_hop(j, bx, bz):
        t, u, v, w = last[j]
        landed((t, u))
        y_2[0] += over_y(zo, bx, PA)
        landed((v, w))
        y_2[1] += over_y(bz, xo, PB)
        sib_2.append(same(blk(zo, bx, GOT, PA), sibling))
        sib_2.append(same(blk(bz, xo, GOT, PB), sibling))

    sib_2, y_2 = [], [[], []]
    for bx, bz, group_a, group_b in zip((xl, xr, xo), (zd, zr, zo), y_a0, y_b0):
        landed(group_a + group_b)
        sib_0 += [same(blk(zl, bx, LACK, PA), sibling), same(blk(bz, x, LACK, PB), sibling)]
    final_hop(0, x, zl)
    ints_copy.wait()
    landed(sib_0)
    hacc[:, 0:256] = part_a(zl)
    hacc[:, 256:512] = part_b(x)
    final_hop(1, xl, zd)
    for bz, bx, group_a, group_b in ((zd, xl, y_1[0], y_1[2]), (zr, xr, y_1[1], y_1[3])):
        landed(group_a + group_b)
        sib_1 += [same(occ.at[bz, :, c, LACK, PA], sibling), same(occ.at[:, bx, c, LACK, PB], sibling)]
    final_hop(2, xr, zr)
    final_hop(3, xo, zo)
    landed(sib_1)
    hacc[:, 0:256] += part_a(zd)
    hacc[:, 256:512] += part_b(xl)
    hacc[:, 0:256] += part_a(zr)
    hacc[:, 256:512] += part_b(xr)
    landed(y_2[0])
    sib_2.append(same(occ.at[zo, :, c, LACK, PA], sibling))
    landed(y_2[1])
    sib_2.append(same(occ.at[:, xo, c, LACK, PB], sibling))
    landed(sib_2)
    h_a = (hacc[:, 0:256] + part_a(zo)).astype(BF16)
    h_b = (hacc[:, 256:512] + part_b(xo)).astype(BF16)
    hrow[x, :, 0:256] = h_a
    hrow[x, :, 256:512] = h_b
    for s in range(3):
        hcol[s, zl, c, :, 0:256] = h_a[64 * s:64 * s + 64]
        hcol[s, zl, c, :, 256:512] = h_b[64 * s:64 * s + 64]

    def columns_out(s):
        return [same(hcol.at[s, zl, c], in_group(d)) for d in (1, 3, 2)]

    UPPER, LOWER = pl.ds(0, 96), pl.ds(96, 96)
    Q = [pl.ds(48 * j, 48) for j in range(4)]
    r_in = [[same(hrow.at[x, UPPER], east), same(hrow.at[x, UPPER], west)]]
    c_in = [columns_out(0)]
    r_in.append([same(hrow.at[x, LOWER], east), same(hrow.at[x, LOWER], west)])
    c_in += [columns_out(1), columns_out(2)]
    c_sib = [[same(hcol.at[s, zl, c], sibling)] for s in range(3)]
    for t in range(2):
        for copy in r_in[t]:
            copy.wait_recv()
        r_in[t] = [same(hrow.at[xl, Q[2 * t]], east), same(hrow.at[xr, Q[2 * t + 1]], west)]

    yr, yl, yo = up(y, 1), up(y, -1), up(y, 2)
    hr, hl, ho = up(zh, 1), up(zh, -1), up(zh, 2)
    z_up, z_dn = at(dz=4), at(dz=-4)
    A, B = pl.ds(0, 192), pl.ds(192, 192)
    TA, TB = pl.ds(0, 48), pl.ds(48, 48)
    y1, y2, xs, z1, z2 = {}, {}, {}, {}, {}

    def columns_in(s):
        for copy, d in zip(c_in[s], (3, 1, 2)):
            copy.wait_recv()
            c_sib[s].append(same(hcol.at[s, up(zl, d), c], sibling))
        for copy in c_sib[s]:
            copy.wait_recv()

    def product(k):
        s, t = k // 2, k % 2
        rows = hrow[:, 96 * t:96 * t + 96].reshape(384, 512)
        for half in range(2):
            cols = hcol[s, 2 * half:2 * half + 2].reshape(256, 512)
            p = lax.dot_general(rows, cols, (((1,), (1,)), ((), ())), preferred_element_type=F32)
            p = p.astype(BF16)
            pb[k, 2 * half] = p[:, 0:128]
            pb[k, 2 * half + 1] = p[:, 128:256]

    def y_first(k):
        if k % 2 == 0:
            columns_in(k // 2)
        if k < 2:
            for copy in r_in[k]:
                copy.wait_recv()
        product(k)
        y1[k] = (send(pb.at[k, yo, A], yin.at[k, 0], y_up),
                 send(pb.at[k, yo, B], yin.at[k, 1], y_dn),
                 send(pb.at[k, yr, B], yin.at[k, 2], y_up),
                 send(pb.at[k, yl, A], yin.at[k, 3], y_dn))

    def y_second(k):
        y1[k][0].wait_recv()
        pb[k, yr, A] = (pb[k, yr, A].astype(F32) + yin[k, 0].astype(F32)).astype(BF16)
        up_copy = send(pb.at[k, yr, A], yin.at[k, 4], y_up)
        y1[k][1].wait_recv()
        pb[k, yl, B] = (pb[k, yl, B].astype(F32) + yin[k, 1].astype(F32)).astype(BF16)
        y2[k] = (up_copy, send(pb.at[k, yl, B], yin.at[k, 5], y_dn))

    def y_last(k):
        for copy in y1[k][2:] + y2[k]:
            copy.wait_recv()
        ysum[k, 0:2] = (pb[k, y, A].astype(F32) + yin[k, 3].astype(F32)
                        + yin[k, 4].astype(F32)).astype(BF16).reshape(2, 96, 128)
        ysum[k, 2:4] = (pb[k, y, B].astype(F32) + yin[k, 2].astype(F32)
                        + yin[k, 5].astype(F32)).astype(BF16).reshape(2, 96, 128)
        xs[k] = [send(ysum.at[k, up(x, d)], xin.at[k, x], at(dx=d)) for d in (2, 1, -1)]
        xin[k, x] = ysum[k, x]

    def z_first(k):
        for copy in xs[k]:
            copy.wait_recv()
        z1[k] = (send(xin.at[k, ho, TA], zin.at[k, 0], z_up),
                 send(xin.at[k, ho, TB], zin.at[k, 1], z_dn),
                 send(xin.at[k, hr, TB], zin.at[k, 2], z_up),
                 send(xin.at[k, hl, TA], zin.at[k, 3], z_dn))

    def z_second(k):
        z1[k][0].wait_recv()
        zbuf[k, 0] = (xin[k, hr, TA].astype(F32) + zin[k, 0].astype(F32)).astype(BF16)
        up_copy = send(zbuf.at[k, 0], zin.at[k, 4], z_up)
        z1[k][1].wait_recv()
        zbuf[k, 1] = (xin[k, hl, TB].astype(F32) + zin[k, 1].astype(F32)).astype(BF16)
        z2[k] = (up_copy, send(zbuf.at[k, 1], zin.at[k, 5], z_dn))

    def z_last(k):
        for copy in z1[k][2:] + z2[k]:
            copy.wait_recv()
        top = xin[k, zh, TA].astype(F32) + zin[k, 3].astype(F32) + zin[k, 4].astype(F32)
        bot = xin[k, zh, TB].astype(F32) + zin[k, 2].astype(F32) + zin[k, 5].astype(F32)
        s, t = k // 2, k % 2
        for first, v in ((96 * t, top), (96 * t + 48, bot)):
            out_ref[first:first + 48, 64 * s:64 * s + 64] = v[:, 0:64]
            out_ref[first:first + 48, 192 + 64 * s:192 + 64 * s + 64] = v[:, 64:128]

    steps = {"F": y_first, "S": y_second, "L": y_last, "f": z_first, "s": z_second, "l": z_last}
    for part in ("F0F1S0F2S1F3L0S2F4", "L1S3F5f0L2f1S4L3S5f2s0L4s1f3L5",
                 "s2l0f4f5s3l1s4l2s5l3l4l5"):
        for j in range(0, len(part), 2):
            steps[part[j]](int(part[j + 1]))
    for copy in copies:
        copy.wait_send()


def local(integrals, occupied):
    return pl.pallas_call(
        kernel,
        out_shape=jax.ShapeDtypeStruct((192, 384), F32),
        in_specs=[pl.BlockSpec(memory_space=pltpu.HBM)] * 2,
        out_specs=pl.BlockSpec(memory_space=pltpu.VMEM),
        scratch_shapes=[
            pltpu.VMEM((4, 4, 2, 192, 512), BF16),
            pltpu.VMEM((192, 6144), BF16),
            pltpu.VMEM((192, 512), F32),
            pltpu.VMEM((4, 192, 512), BF16),
            pltpu.VMEM((3, 4, 2, 64, 512), BF16),
            pltpu.VMEM((6, 4, 384, 128), BF16),
            pltpu.VMEM((6, 6, 192, 128), BF16),
            pltpu.VMEM((6, 4, 96, 128), BF16),
            pltpu.VMEM((6, 4, 96, 128), BF16),
            pltpu.VMEM((6, 6, 48, 128), BF16),
            pltpu.VMEM((6, 2, 48, 128), BF16),
            pltpu.SemaphoreType.DMA((N_SEM,)),
            pltpu.SemaphoreType.DMA((N_SEM,)),
            pltpu.SemaphoreType.DMA((2,)),
        ],
        compiler_params=pltpu.CompilerParams(
            collective_id=0, has_side_effects=True, vmem_limit_bytes=60 << 20),
        name="exchange",
    )(integrals.reshape(192, 6144), occupied)


def solution(mesh):
    in_specs = (P("grp", "row", None), P("row", None))
    return jax.shard_map(local, mesh=mesh, in_specs=in_specs, out_specs=P("row", "grp"), check_vma=False)
```

```python
import jax
import jax.numpy as jnp
from jax import lax
from jax.experimental import pallas as pl
from jax.experimental.pallas import tpu as pltpu
from jax.sharding import PartitionSpec as P

MESH = pl.DeviceIdType.MESH
F32 = jnp.float32
BF16 = jnp.bfloat16

N_SEM = 73


def kernel(ints_hbm, occ_hbm, out_ref, occ, ints, hacc, hrow, hcol, pb,
           yin, ysum, xin, zin, zbuf, ssem, rsem, lsem):
    grp, row = lax.axis_index("grp"), lax.axis_index("row")
    y, zh = grp // 4, grp % 4
    zl, x, c = row // 8, (row // 2) % 4, row % 2
    z = zh * 4 + zl

    def up(v, d, n=4):
        return (v + d + n) % n

    def at(dx=0, dy=0, dz=0):
        zz = up(z, dz, 16)
        return (up(y, dy) * 4 + zz // 4, (zz % 4) * 8 + up(x, dx) * 2 + c)

    def in_group(d):
        return (grp, up(zl, d) * 8 + x * 2 + c)

    sibling = (grp, zl * 8 + x * 2 + (1 - c))

    made = [0]

    def arrival():
        made[0] += 1
        return made[0] - 1

    def send(src, dst, to, sem, group):
        pltpu.make_async_remote_copy(
            src_ref=src, dst_ref=dst, send_sem=ssem.at[group], recv_sem=rsem.at[sem],
            device_id=to, device_id_type=MESH).start()
        return sem

    def same(ref, to, sem, group):
        return send(ref, ref, to, sem, group)

    def waiting(ref, sem, group):
        return pltpu.make_async_remote_copy(
            src_ref=ref, dst_ref=ref, send_sem=ssem.at[group], recv_sem=rsem.at[sem],
            device_id=sibling, device_id_type=MESH)

    def landed(sem, ref):
        waiting(ref, sem, 0).wait_recv()

    own_copy = pltpu.make_async_copy(occ_hbm, occ.at[zl, x, c], lsem.at[0])
    own_copy.start()
    ints_copy = pltpu.make_async_copy(ints_hbm, ints, lsem.at[1])
    ints_copy.start()

    barrier = pltpu.get_barrier_semaphore()
    partners = [sibling, at(dx=1), at(dx=2), at(dx=-1), at(dy=1), at(dy=-1), at(dz=1), at(dz=-1),
                at(dz=4), at(dz=-4), in_group(1), in_group(2), in_group(3)]
    for partner in partners:
        pl.semaphore_signal(barrier, inc=1, device_id=partner, device_id_type=MESH)
    pl.semaphore_wait(barrier, len(partners))
    own_copy.wait()

    xr, xl, xo = up(x, 1), up(x, -1), up(x, 2)
    zr, zd, zo = up(zl, 1), up(zl, -1), up(zl, 2)
    east, west, north, south = at(dx=1), at(dx=-1), at(dz=1), at(dz=-1)
    PA, PB = pl.ds(0, 256), pl.ds(256, 256)
    ALL, TOP, BOT = pl.ds(0, 192), pl.ds(0, 96), pl.ds(96, 96)

    def blk(bz, bx, rows, cols):
        return occ.at[bz, bx, c, rows, cols]

    GATHER, SIBLING, BLOCKS, SUMS = range(4)
    half_block = blk(zl, x, ALL, PA)

    def hop(ref, to, sem=None):
        return same(ref, to, arrival() if sem is None else sem, GATHER)

    def over(ref, sem):
        return same(ref, sibling, sem, SIBLING)

    sib_0, sib_1, sib_2 = arrival(), arrival(), arrival()
    fwd_a = [[], []]
    fwd_b = [[], []]
    own_a, own_b = blk(zl, x, ALL, PA), blk(zl, x, ALL, PB)
    a_e, a_w = hop(own_a, east), hop(own_a, west)
    b_n, b_s = hop(own_b, north), hop(own_b, south)
    fwd_a[0].append(hop(own_a, north))
    fwd_a[1].append(hop(own_a, south))
    fwd_b[0].append(hop(own_b, east))
    fwd_b[1].append(hop(own_b, west))
    over(occ.at[zl, x, c], sib_0)

    a_2, b_2 = arrival(), arrival()
    landed(a_e, half_block)
    hop(blk(zl, xl, TOP, PA), east, a_2)
    fwd_a[0].append(hop(blk(zl, xl, ALL, PA), north))
    fwd_a[1].append(hop(blk(zl, xl, ALL, PA), south))
    landed(b_n, half_block)
    hop(blk(zd, x, TOP, PB), north, b_2)
    fwd_b[0].append(hop(blk(zd, x, ALL, PB), east))
    fwd_b[1].append(hop(blk(zd, x, ALL, PB), west))
    landed(a_w, half_block)
    hop(blk(zl, xr, BOT, PA), west, a_2)
    fwd_a[0].append(hop(blk(zl, xr, ALL, PA), north))
    fwd_a[1].append(hop(blk(zl, xr, ALL, PA), south))
    landed(b_s, half_block)
    hop(blk(zr, x, BOT, PB), south, b_2)
    fwd_b[0].append(hop(blk(zr, x, ALL, PB), east))
    fwd_b[1].append(hop(blk(zr, x, ALL, PB), west))
    over(blk(zl, xl, ALL, PA), sib_0)
    over(blk(zl, xr, ALL, PA), sib_0)
    over(blk(zd, x, ALL, PB), sib_0)
    over(blk(zr, x, ALL, PB), sib_0)
    landed(a_2, half_block)
    fwd_a[0].append(hop(blk(zl, xo, ALL, PA), north))
    fwd_a[1].append(hop(blk(zl, xo, ALL, PA), south))
    over(blk(zl, xo, ALL, PA), sib_0)
    landed(b_2, half_block)
    fwd_b[0].append(hop(blk(zo, x, ALL, PB), east))
    fwd_b[1].append(hop(blk(zo, x, ALL, PB), west))
    over(blk(zo, x, ALL, PB), sib_0)

    last = []
    for bx, bz, j in zip((x, xl, xr, xo), (zl, zd, zr, zo), range(4)):
        last_a, last_b = arrival(), arrival()
        landed(fwd_a[0][j], half_block)
        hop(blk(zd, bx, TOP, PA), north, last_a)
        over(blk(zd, bx, ALL, PA), sib_1)
        landed(fwd_a[1][j], half_block)
        hop(blk(zr, bx, BOT, PA), south, last_a)
        over(blk(zr, bx, ALL, PA), sib_1)
        landed(fwd_b[0][j], half_block)
        hop(blk(bz, xl, TOP, PB), east, last_b)
        over(blk(bz, xl, ALL, PB), sib_1)
        landed(fwd_b[1][j], half_block)
        hop(blk(bz, xr, BOT, PB), west, last_b)
        over(blk(bz, xr, ALL, PB), sib_1)
        last.append((last_a, bx, last_b, bz))

    def lanes(start, size):
        return pl.ds(pl.multiple_of(start, 128), size)

    def part_a(bz):
        return jnp.dot(ints[:, lanes(bz * 1536, 1536)],
                       occ[bz, :, :, :, 0:256].reshape(1536, 256), preferred_element_type=F32)

    def part_b(bx):
        total = None
        for bz in range(4):
            term = jnp.dot(ints[:, lanes(bz * 1536 + bx * 384, 384)],
                           occ[bz, bx, :, :, 256:512].reshape(384, 256), preferred_element_type=F32)
            total = term if total is None else total + term
        return total

    ints_copy.wait()
    landed(sib_0, occ.at[zl, :, 1 - c])
    hacc[:, 0:256] = part_a(zl)
    hacc[:, 256:512] = part_b(x)
    landed(sib_1, occ.at[zl])
    hacc[:, 0:256] += part_a(zd)
    hacc[:, 256:512] += part_b(xl)
    hacc[:, 0:256] += part_a(zr)
    hacc[:, 256:512] += part_b(xr)
    for last_a, bx, last_b, bz in last:
        landed(last_a, half_block)
        over(blk(zo, bx, ALL, PA), sib_2)
        landed(last_b, half_block)
        over(blk(bz, xo, ALL, PB), sib_2)
    landed(sib_2, occ.at[zl, :, 1 - c])
    h_a = (hacc[:, 0:256] + part_a(zo)).astype(BF16)
    h_b = (hacc[:, 256:512] + part_b(xo)).astype(BF16)
    hrow[x, :, 0:256] = h_a
    hrow[x, :, 256:512] = h_b
    for s in range(3):
        hcol[s, zl, c, :, 0:256] = h_a[64 * s:64 * s + 64]
        hcol[s, zl, c, :, 256:512] = h_b[64 * s:64 * s + 64]

    def columns_out(s):
        sem = arrival()
        for d in (1, 3, 2):
            same(hcol.at[s, zl, c], in_group(d), sem, BLOCKS)
        return sem

    Q = [pl.ds(48 * j, 48) for j in range(4)]
    r_1, r_2 = [arrival(), arrival()], [arrival(), arrival()]
    same(hrow.at[x, TOP], east, r_1[0], BLOCKS)
    same(hrow.at[x, TOP], west, r_1[0], BLOCKS)
    c_in = [columns_out(0)]
    same(hrow.at[x, BOT], east, r_1[1], BLOCKS)
    same(hrow.at[x, BOT], west, r_1[1], BLOCKS)
    c_in += [columns_out(1), columns_out(2)]
    c_sib = [arrival() for s in range(3)]
    for s in range(3):
        same(hcol.at[s, zl, c], sibling, c_sib[s], BLOCKS)
    for t in range(2):
        landed(r_1[t], hrow.at[x])
        same(hrow.at[xl, Q[2 * t]], east, r_2[t], BLOCKS)
        same(hrow.at[xr, Q[2 * t + 1]], west, r_2[t], BLOCKS)

    yr, yl, yo = up(y, 1), up(y, -1), up(y, 2)
    y_up, y_dn = at(dy=1), at(dy=-1)
    hr, hl, ho = up(zh, 1), up(zh, -1), up(zh, 2)
    z_up, z_dn = at(dz=4), at(dz=-4)
    A, B = pl.ds(0, 192), pl.ds(192, 192)
    TA, TB = pl.ds(0, 48), pl.ds(48, 48)
    y1, y2, xs, z1, z2 = {}, {}, {}, {}, {}

    def columns_in(s):
        landed(c_in[s], hcol.at[s, 0:3, c])
        for d in (1, 3, 2):
            same(hcol.at[s, up(zl, d), c], sibling, c_sib[s], BLOCKS)
        landed(c_sib[s], hcol.at[s, :, 1 - c])

    def product(k):
        s, t = k // 2, k % 2
        rows = hrow[:, 96 * t:96 * t + 96].reshape(384, 512)
        for half in range(2):
            cols = hcol[s, 2 * half:2 * half + 2].reshape(256, 512)
            p = lax.dot_general(rows, cols, (((1,), (1,)), ((), ())), preferred_element_type=F32)
            p = p.astype(BF16)
            pb[k, 2 * half] = p[:, 0:128]
            pb[k, 2 * half + 1] = p[:, 128:256]

    def pass_on(src, dst, to, sem):
        send(src, dst, to, sem, SUMS)

    def y_first(k):
        if k % 2 == 0:
            columns_in(k // 2)
        if k < 2:
            landed(r_2[k], hrow.at[x, TOP])
        product(k)
        y1[k], y2[k] = arrival(), arrival()
        pass_on(pb.at[k, yo, A], yin.at[k, 0], y_up, y1[k])
        pass_on(pb.at[k, yo, B], yin.at[k, 1], y_dn, y1[k])
        pass_on(pb.at[k, yr, B], yin.at[k, 2], y_up, y2[k])
        pass_on(pb.at[k, yl, A], yin.at[k, 3], y_dn, y2[k])

    def y_second(k):
        landed(y1[k], yin.at[k, 0:2])
        pb[k, yr, A] = (pb[k, yr, A].astype(F32) + yin[k, 0].astype(F32)).astype(BF16)
        pass_on(pb.at[k, yr, A], yin.at[k, 4], y_up, y2[k])
        pb[k, yl, B] = (pb[k, yl, B].astype(F32) + yin[k, 1].astype(F32)).astype(BF16)
        pass_on(pb.at[k, yl, B], yin.at[k, 5], y_dn, y2[k])

    def y_last(k):
        landed(y2[k], yin.at[k, 2:6])
        ysum[k, 0:2] = (pb[k, y, A].astype(F32) + yin[k, 3].astype(F32)
                        + yin[k, 4].astype(F32)).astype(BF16).reshape(2, 96, 128)
        ysum[k, 2:4] = (pb[k, y, B].astype(F32) + yin[k, 2].astype(F32)
                        + yin[k, 5].astype(F32)).astype(BF16).reshape(2, 96, 128)
        xs[k] = arrival()
        for d in (2, 1, -1):
            pass_on(ysum.at[k, up(x, d)], xin.at[k, x], at(dx=d), xs[k])
        xin[k, x] = ysum[k, x]

    def z_first(k):
        landed(xs[k], xin.at[k, 0:3])
        z1[k], z2[k] = arrival(), arrival()
        pass_on(xin.at[k, ho, TA], zin.at[k, 0], z_up, z1[k])
        pass_on(xin.at[k, ho, TB], zin.at[k, 1], z_dn, z1[k])
        pass_on(xin.at[k, hr, TB], zin.at[k, 2], z_up, z2[k])
        pass_on(xin.at[k, hl, TA], zin.at[k, 3], z_dn, z2[k])

    def z_second(k):
        landed(z1[k], zin.at[k, 0:2])
        zbuf[k, 0] = (xin[k, hr, TA].astype(F32) + zin[k, 0].astype(F32)).astype(BF16)
        pass_on(zbuf.at[k, 0], zin.at[k, 4], z_up, z2[k])
        zbuf[k, 1] = (xin[k, hl, TB].astype(F32) + zin[k, 1].astype(F32)).astype(BF16)
        pass_on(zbuf.at[k, 1], zin.at[k, 5], z_dn, z2[k])

    def z_last(k):
        landed(z2[k], zin.at[k, 2:6])
        top = xin[k, zh, TA].astype(F32) + zin[k, 3].astype(F32) + zin[k, 4].astype(F32)
        bot = xin[k, zh, TB].astype(F32) + zin[k, 2].astype(F32) + zin[k, 5].astype(F32)
        s, t = k // 2, k % 2
        for first, v in ((96 * t, top), (96 * t + 48, bot)):
            out_ref[first:first + 48, 64 * s:64 * s + 64] = v[:, 0:64]
            out_ref[first:first + 48, 192 + 64 * s:192 + 64 * s + 64] = v[:, 64:128]

    steps = {"F": y_first, "S": y_second, "L": y_last, "f": z_first, "s": z_second, "l": z_last}
    for part in ("F0F1S0F2S1F3L0S2F4", "L1S3F5f0L2f1S4L3S5f2s0L4s1f3L5",
                 "s2l0f4f5s3l1s4l2s5l3l4l5"):
        for j in range(0, len(part), 2):
            steps[part[j]](int(part[j + 1]))
    for group, ref in ((GATHER, occ.at[0:3, 0:3, :, 0:160]), (SIBLING, occ.at[:, :, 0]),
                       (BLOCKS, occ.at[0:3, :, 0, 0:160]), (SUMS, occ.at[0:3, 0:3, :, 0:144])):
        waiting(ref, 0, group).wait_send()
    assert made[0] == N_SEM, made[0]


def local(integrals, occupied):
    return pl.pallas_call(
        kernel,
        out_shape=jax.ShapeDtypeStruct((192, 384), F32),
        in_specs=[pl.BlockSpec(memory_space=pltpu.HBM)] * 2,
        out_specs=pl.BlockSpec(memory_space=pltpu.VMEM),
        scratch_shapes=[
            pltpu.VMEM((4, 4, 2, 192, 512), BF16),
            pltpu.VMEM((192, 6144), BF16),
            pltpu.VMEM((192, 512), F32),
            pltpu.VMEM((4, 192, 512), BF16),
            pltpu.VMEM((3, 4, 2, 64, 512), BF16),
            pltpu.VMEM((6, 4, 384, 128), BF16),
            pltpu.VMEM((6, 6, 192, 128), BF16),
            pltpu.VMEM((6, 4, 96, 128), BF16),
            pltpu.VMEM((6, 4, 96, 128), BF16),
            pltpu.VMEM((6, 6, 48, 128), BF16),
            pltpu.VMEM((6, 2, 48, 128), BF16),
            pltpu.SemaphoreType.DMA((4,)),
            pltpu.SemaphoreType.DMA((N_SEM,)),
            pltpu.SemaphoreType.DMA((2,)),
        ],
        compiler_params=pltpu.CompilerParams(
            collective_id=0, has_side_effects=True, vmem_limit_bytes=60 << 20),
        name="exchange",
    )(integrals.reshape(192, 6144), occupied)


def solution(mesh):
    in_specs = (P("grp", "row", None), P("row", None))
    return jax.shard_map(local, mesh=mesh, in_specs=in_specs, out_specs=P("row", "grp"), check_vma=False)
```

```python
import jax
import jax.numpy as jnp
from jax import lax
from jax.experimental import pallas as pl
from jax.experimental.pallas import tpu as pltpu
from jax.sharding import PartitionSpec as P

MESH = pl.DeviceIdType.MESH
F32 = jnp.float32
BF16 = jnp.bfloat16

N_SEM = 78


def kernel(ints_hbm, occ_hbm, out_ref, occ, ints, hacc, hrow, hcol, pb,
           yin, ysum, xin, zin, zbuf, ssem, rsem, lsem):
    grp, row = lax.axis_index("grp"), lax.axis_index("row")
    y, zh = grp // 4, grp % 4
    zl, x, c = row // 8, (row // 2) % 4, row % 2
    z = zh * 4 + zl

    def up(v, d, n=4):
        return (v + d + n) % n

    def at(dx=0, dy=0, dz=0):
        zz = up(z, dz, 16)
        return (up(y, dy) * 4 + zz // 4, (zz % 4) * 8 + up(x, dx) * 2 + c)

    def in_group(d):
        return (grp, up(zl, d) * 8 + x * 2 + c)

    sibling = (grp, zl * 8 + x * 2 + (1 - c))

    made = [0]

    def arrival():
        made[0] += 1
        return made[0] - 1

    def send(src, dst, to, sem, group):
        pltpu.make_async_remote_copy(
            src_ref=src, dst_ref=dst, send_sem=ssem.at[group], recv_sem=rsem.at[sem],
            device_id=to, device_id_type=MESH).start()
        return sem

    def same(ref, to, sem, group):
        return send(ref, ref, to, sem, group)

    def waiting(ref, sem, group):
        return pltpu.make_async_remote_copy(
            src_ref=ref, dst_ref=ref, send_sem=ssem.at[group], recv_sem=rsem.at[sem],
            device_id=sibling, device_id_type=MESH)

    def landed(sem, ref):
        waiting(ref, sem, 0).wait_recv()

    own_copy = pltpu.make_async_copy(occ_hbm, occ.at[zl, x, c], lsem.at[0])
    own_copy.start()
    ints_copy = pltpu.make_async_copy(ints_hbm, ints, lsem.at[1])
    ints_copy.start()

    barrier = pltpu.get_barrier_semaphore()
    partners = [sibling, at(dx=1), at(dx=2), at(dx=-1), at(dy=1), at(dy=-1), at(dz=1), at(dz=-1),
                at(dz=4), at(dz=-4), in_group(1), in_group(2), in_group(3)]
    for partner in partners:
        pl.semaphore_signal(barrier, inc=1, device_id=partner, device_id_type=MESH)
    pl.semaphore_wait(barrier, len(partners))
    own_copy.wait()

    xr, xl, xo = up(x, 1), up(x, -1), up(x, 2)
    zr, zd, zo = up(zl, 1), up(zl, -1), up(zl, 2)
    east, west, north, south = at(dx=1), at(dx=-1), at(dz=1), at(dz=-1)
    PA, PB = pl.ds(0, 256), pl.ds(256, 256)
    y_up, y_dn = at(dy=1), at(dy=-1)
    odd = y % 2

    def rows_at(first, step, size):
        return pl.ds(pl.multiple_of(first + step * odd, 32), size)

    GOT, TOP, BOT = rows_at(0, 64, 128), rows_at(0, 64, 64), rows_at(64, 64, 64)
    LACK, LACK_TOP, LACK_BOT = rows_at(128, -128, 64), rows_at(128, -128, 32), rows_at(160, -128, 32)
    UP, DOWN = rows_at(0, 160, 32), rows_at(32, 96, 32)

    def blk(bz, bx, rows, cols):
        return occ.at[bz, bx, c, rows, cols]

    GATHER, SIBLING, BLOCKS, SUMS = range(4)
    got_block = blk(zl, x, GOT, PA)

    def hop(ref, to, sem=None):
        return same(ref, to, arrival() if sem is None else sem, GATHER)

    def over(ref, sem):
        return same(ref, sibling, sem, SIBLING)

    def over_y(bz, bx, cols, sem):
        hop(blk(bz, bx, UP, cols), y_up, sem)
        hop(blk(bz, bx, DOWN, cols), y_dn, sem)

    sib_0, sib_1, sib_2 = arrival(), arrival(), arrival()
    y_0, y_1 = arrival(), [arrival() for i in range(4)]
    fwd_a = [[], []]
    fwd_b = [[], []]
    own_a, own_b = blk(zl, x, GOT, PA), blk(zl, x, GOT, PB)
    a_e, a_w = hop(own_a, east), hop(own_a, west)
    b_n, b_s = hop(own_b, north), hop(own_b, south)
    fwd_a[0].append(hop(own_a, north))
    fwd_a[1].append(hop(own_a, south))
    fwd_b[0].append(hop(own_b, east))
    fwd_b[1].append(hop(own_b, west))
    over(occ.at[zl, x, c], sib_0)

    a_2, b_2 = arrival(), arrival()
    landed(a_e, got_block)
    hop(blk(zl, xl, TOP, PA), east, a_2)
    over_y(zl, xl, PA, y_0)
    fwd_a[0].append(hop(blk(zl, xl, GOT, PA), north))
    fwd_a[1].append(hop(blk(zl, xl, GOT, PA), south))
    landed(b_n, got_block)
    hop(blk(zd, x, TOP, PB), north, b_2)
    over_y(zd, x, PB, y_0)
    fwd_b[0].append(hop(blk(zd, x, GOT, PB), east))
    fwd_b[1].append(hop(blk(zd, x, GOT, PB), west))
    landed(a_w, got_block)
    hop(blk(zl, xr, BOT, PA), west, a_2)
    over_y(zl, xr, PA, y_0)
    fwd_a[0].append(hop(blk(zl, xr, GOT, PA), north))
    fwd_a[1].append(hop(blk(zl, xr, GOT, PA), south))
    landed(b_s, got_block)
    hop(blk(zr, x, BOT, PB), south, b_2)
    over_y(zr, x, PB, y_0)
    fwd_b[0].append(hop(blk(zr, x, GOT, PB), east))
    fwd_b[1].append(hop(blk(zr, x, GOT, PB), west))
    over(blk(zl, xl, GOT, PA), sib_0)
    over(blk(zl, xr, GOT, PA), sib_0)
    over(blk(zd, x, GOT, PB), sib_0)
    over(blk(zr, x, GOT, PB), sib_0)
    landed(a_2, got_block)
    fwd_a[0].append(hop(blk(zl, xo, GOT, PA), north))
    fwd_a[1].append(hop(blk(zl, xo, GOT, PA), south))
    over_y(zl, xo, PA, y_0)
    over(blk(zl, xo, GOT, PA), sib_0)
    landed(b_2, got_block)
    fwd_b[0].append(hop(blk(zo, x, GOT, PB), east))
    fwd_b[1].append(hop(blk(zo, x, GOT, PB), west))
    over_y(zo, x, PB, y_0)
    over(blk(zo, x, GOT, PB), sib_0)

    last = []
    for bx, bz, j in zip((x, xl, xr, xo), (zl, zd, zr, zo), range(4)):
        last_a, last_b = arrival(), arrival()
        landed(fwd_a[0][j], got_block)
        hop(blk(zd, bx, TOP, PA), north, last_a)
        over_y(zd, bx, PA, y_1[0])
        landed(fwd_b[0][j], got_block)
        hop(blk(bz, xl, TOP, PB), east, last_b)
        over_y(bz, xl, PB, y_1[1])
        landed(fwd_a[1][j], got_block)
        hop(blk(zr, bx, BOT, PA), south, last_a)
        over_y(zr, bx, PA, y_1[2])
        landed(fwd_b[1][j], got_block)
        hop(blk(bz, xr, BOT, PB), west, last_b)
        over_y(bz, xr, PB, y_1[3])
        over(blk(zd, bx, GOT, PA), sib_1)
        over(blk(bz, xl, GOT, PB), sib_1)
        over(blk(zr, bx, GOT, PA), sib_1)
        over(blk(bz, xr, GOT, PB), sib_1)
        last.append((last_a, bx, last_b, bz))

    landed(y_0, occ.at[0, :, 0, 0:48])
    for bx, bz in zip((xl, xr, xo), (zd, zr, zo)):
        over(blk(zl, bx, LACK, PA), sib_0)
        over(blk(bz, x, LACK, PB), sib_0)
    lack_a, lack_b = arrival(), arrival()
    quarter = occ.at[zl, :, c, LACK, PA]
    for i, (part, top, bot, to, sem) in enumerate((
            (lambda rows: occ.at[zd, :, c, rows, PA], LACK_TOP, None, north, lack_a),
            (lambda rows: occ.at[:, xl, c, rows, PB], LACK_TOP, None, east, lack_b),
            (lambda rows: occ.at[zr, :, c, rows, PA], None, LACK_BOT, south, lack_a),
            (lambda rows: occ.at[:, xr, c, rows, PB], None, LACK_BOT, west, lack_b))):
        landed(y_1[i], quarter)
        hop(part(top or bot), to, sem)
        over(part(LACK), sib_1)

    def lanes(start, size):
        return pl.ds(pl.multiple_of(start, 128), size)

    def part_a(bz):
        return jnp.dot(ints[:, lanes(bz * 1536, 1536)],
                       occ[bz, :, :, :, 0:256].reshape(1536, 256), preferred_element_type=F32)

    def part_b(bx):
        total = None
        for bz in range(4):
            term = jnp.dot(ints[:, lanes(bz * 1536 + bx * 384, 384)],
                           occ[bz, bx, :, :, 256:512].reshape(384, 256), preferred_element_type=F32)
            total = term if total is None else total + term
        return total

    for last_a, bx, last_b, bz in last:
        landed(last_a, got_block)
        over(blk(zo, bx, GOT, PA), sib_2)
        landed(last_b, got_block)
        over(blk(bz, xo, GOT, PB), sib_2)
    ints_copy.wait()
    landed(sib_0, occ.at[zl, :, 1 - c])
    hacc[:, 0:256] = part_a(zl)
    hacc[:, 256:512] = part_b(x)
    landed(lack_a, quarter)
    over(occ.at[zo, :, c, LACK, PA], sib_2)
    landed(lack_b, quarter)
    over(occ.at[:, xo, c, LACK, PB], sib_2)
    landed(sib_1, occ.at[zl])
    hacc[:, 0:256] += part_a(zd)
    hacc[:, 256:512] += part_b(xl)
    hacc[:, 0:256] += part_a(zr)
    hacc[:, 256:512] += part_b(xr)
    landed(sib_2, occ.at[zl, :, 1 - c])
    h_a = (hacc[:, 0:256] + part_a(zo)).astype(BF16)
    h_b = (hacc[:, 256:512] + part_b(xo)).astype(BF16)
    hrow[x, :, 0:256] = h_a
    hrow[x, :, 256:512] = h_b
    for s in range(3):
        hcol[s, zl, c, :, 0:256] = h_a[64 * s:64 * s + 64]
        hcol[s, zl, c, :, 256:512] = h_b[64 * s:64 * s + 64]

    def columns_out(s):
        sem = arrival()
        for d in (1, 3, 2):
            same(hcol.at[s, zl, c], in_group(d), sem, BLOCKS)
        return sem

    UPPER, LOWER = pl.ds(0, 96), pl.ds(96, 96)
    r_in = [arrival(), arrival()]
    c_in = []
    for t, half in enumerate((UPPER, LOWER)):
        for d in (2, 1, -1):
            same(hrow.at[x, half], at(dx=d), r_in[t], BLOCKS)
        c_in.append(columns_out(t))
    c_in.append(columns_out(2))
    c_sib = [arrival() for s in range(3)]
    for s in range(3):
        same(hcol.at[s, zl, c], sibling, c_sib[s], BLOCKS)

    yr, yl, yo = up(y, 1), up(y, -1), up(y, 2)
    hr, hl, ho = up(zh, 1), up(zh, -1), up(zh, 2)
    z_up, z_dn = at(dz=4), at(dz=-4)
    A, B = pl.ds(0, 192), pl.ds(192, 192)
    TA, TB = pl.ds(0, 48), pl.ds(48, 48)
    y1, y2, xs, z1, z2 = {}, {}, {}, {}, {}

    def columns_in(s):
        landed(c_in[s], hcol.at[s, 0:3, c])
        for d in (1, 3, 2):
            same(hcol.at[s, up(zl, d), c], sibling, c_sib[s], BLOCKS)
        landed(c_sib[s], hcol.at[s, :, 1 - c])

    def product(k):
        s, t = k // 2, k % 2
        rows = hrow[:, 96 * t:96 * t + 96].reshape(384, 512)
        for half in range(2):
            cols = hcol[s, 2 * half:2 * half + 2].reshape(256, 512)
            p = lax.dot_general(rows, cols, (((1,), (1,)), ((), ())), preferred_element_type=F32)
            p = p.astype(BF16)
            pb[k, 2 * half] = p[:, 0:128]
            pb[k, 2 * half + 1] = p[:, 128:256]

    def pass_on(src, dst, to, sem):
        send(src, dst, to, sem, SUMS)

    def y_first(k):
        if k % 2 == 0:
            columns_in(k // 2)
        if k < 2:
            landed(r_in[k], hrow.at[0:3, UPPER])
        product(k)
        y1[k], y2[k] = arrival(), arrival()
        pass_on(pb.at[k, yo, A], yin.at[k, 0], y_up, y1[k])
        pass_on(pb.at[k, yo, B], yin.at[k, 1], y_dn, y1[k])
        pass_on(pb.at[k, yr, B], yin.at[k, 2], y_up, y2[k])
        pass_on(pb.at[k, yl, A], yin.at[k, 3], y_dn, y2[k])

    def y_second(k):
        landed(y1[k], yin.at[k, 0:2])
        pb[k, yr, A] = (pb[k, yr, A].astype(F32) + yin[k, 0].astype(F32)).astype(BF16)
        pass_on(pb.at[k, yr, A], yin.at[k, 4], y_up, y2[k])
        pb[k, yl, B] = (pb[k, yl, B].astype(F32) + yin[k, 1].astype(F32)).astype(BF16)
        pass_on(pb.at[k, yl, B], yin.at[k, 5], y_dn, y2[k])

    def y_last(k):
        landed(y2[k], yin.at[k, 2:6])
        ysum[k, 0:2] = (pb[k, y, A].astype(F32) + yin[k, 3].astype(F32)
                        + yin[k, 4].astype(F32)).astype(BF16).reshape(2, 96, 128)
        ysum[k, 2:4] = (pb[k, y, B].astype(F32) + yin[k, 2].astype(F32)
                        + yin[k, 5].astype(F32)).astype(BF16).reshape(2, 96, 128)
        xs[k] = arrival()
        for d in (2, 1, -1):
            pass_on(ysum.at[k, up(x, d)], xin.at[k, x], at(dx=d), xs[k])
        xin[k, x] = ysum[k, x]

    def z_first(k):
        landed(xs[k], xin.at[k, 0:3])
        z1[k], z2[k] = arrival(), arrival()
        pass_on(xin.at[k, ho, TA], zin.at[k, 0], z_up, z1[k])
        pass_on(xin.at[k, ho, TB], zin.at[k, 1], z_dn, z1[k])
        pass_on(xin.at[k, hr, TB], zin.at[k, 2], z_up, z2[k])
        pass_on(xin.at[k, hl, TA], zin.at[k, 3], z_dn, z2[k])

    def z_second(k):
        landed(z1[k], zin.at[k, 0:2])
        zbuf[k, 0] = (xin[k, hr, TA].astype(F32) + zin[k, 0].astype(F32)).astype(BF16)
        pass_on(zbuf.at[k, 0], zin.at[k, 4], z_up, z2[k])
        zbuf[k, 1] = (xin[k, hl, TB].astype(F32) + zin[k, 1].astype(F32)).astype(BF16)
        pass_on(zbuf.at[k, 1], zin.at[k, 5], z_dn, z2[k])

    def z_last(k):
        landed(z2[k], zin.at[k, 2:6])
        top = xin[k, zh, TA].astype(F32) + zin[k, 3].astype(F32) + zin[k, 4].astype(F32)
        bot = xin[k, zh, TB].astype(F32) + zin[k, 2].astype(F32) + zin[k, 5].astype(F32)
        s, t = k // 2, k % 2
        for first, v in ((96 * t, top), (96 * t + 48, bot)):
            out_ref[first:first + 48, 64 * s:64 * s + 64] = v[:, 0:64]
            out_ref[first:first + 48, 192 + 64 * s:192 + 64 * s + 64] = v[:, 64:128]

    steps = {"F": y_first, "S": y_second, "L": y_last, "f": z_first, "s": z_second, "l": z_last}
    for part in ("F0F1S0F2S1F3L0S2F4", "L1S3F5f0L2f1S4L3S5f2s0L4s1f3L5",
                 "s2l0f4f5s3l1s4l2s5l3l4l5"):
        for j in range(0, len(part), 2):
            steps[part[j]](int(part[j + 1]))
    for group, ref in ((GATHER, occ.at[0:3, 0:3, :, 0:160]), (SIBLING, occ.at[:, :, 0]),
                       (BLOCKS, occ.at[0:3, :, 0, 0:160]), (SUMS, occ.at[0:3, 0:3, :, 0:144])):
        waiting(ref, 0, group).wait_send()
    assert made[0] == N_SEM, made[0]


def local(integrals, occupied):
    return pl.pallas_call(
        kernel,
        out_shape=jax.ShapeDtypeStruct((192, 384), F32),
        in_specs=[pl.BlockSpec(memory_space=pltpu.HBM)] * 2,
        out_specs=pl.BlockSpec(memory_space=pltpu.VMEM),
        scratch_shapes=[
            pltpu.VMEM((4, 4, 2, 192, 512), BF16),
            pltpu.VMEM((192, 6144), BF16),
            pltpu.VMEM((192, 512), F32),
            pltpu.VMEM((4, 192, 512), BF16),
            pltpu.VMEM((3, 4, 2, 64, 512), BF16),
            pltpu.VMEM((6, 4, 384, 128), BF16),
            pltpu.VMEM((6, 6, 192, 128), BF16),
            pltpu.VMEM((6, 4, 96, 128), BF16),
            pltpu.VMEM((6, 4, 96, 128), BF16),
            pltpu.VMEM((6, 6, 48, 128), BF16),
            pltpu.VMEM((6, 2, 48, 128), BF16),
            pltpu.SemaphoreType.DMA((4,)),
            pltpu.SemaphoreType.DMA((N_SEM,)),
            pltpu.SemaphoreType.DMA((2,)),
        ],
        compiler_params=pltpu.CompilerParams(
            collective_id=0, has_side_effects=True, vmem_limit_bytes=60 << 20),
        name="exchange",
    )(integrals.reshape(192, 6144), occupied)


def solution(mesh):
    in_specs = (P("grp", "row", None), P("row", None))
    return jax.shard_map(local, mesh=mesh, in_specs=in_specs, out_specs=P("row", "grp"), check_vma=False)
```

```python
import jax
import jax.numpy as jnp
from jax import lax
from jax.experimental import pallas as pl
from jax.experimental.pallas import tpu as pltpu
from jax.sharding import PartitionSpec as P

MESH = pl.DeviceIdType.MESH
F32 = jnp.float32
BF16 = jnp.bfloat16

N_SEM = 71


def kernel(ints_hbm, occ_hbm, out_ref, occ, ints, hacc, hrow, hcol, pb,
           yin, ysum, xin, zin, zbuf, ssem, rsem, lsem):
    grp, row = lax.axis_index("grp"), lax.axis_index("row")
    y, zh = grp // 4, grp % 4
    zl, x, c = row // 8, (row // 2) % 4, row % 2
    z = zh * 4 + zl

    def up(v, d, n=4):
        return (v + d + n) % n

    def at(dx=0, dy=0, dz=0):
        zz = up(z, dz, 16)
        return (up(y, dy) * 4 + zz // 4, (zz % 4) * 8 + up(x, dx) * 2 + c)

    def in_group(d):
        return (grp, up(zl, d) * 8 + x * 2 + c)

    sibling = (grp, zl * 8 + x * 2 + (1 - c))

    made = [0]

    def arrival():
        made[0] += 1
        return made[0] - 1

    def send(src, dst, to, sem, group):
        pltpu.make_async_remote_copy(
            src_ref=src, dst_ref=dst, send_sem=ssem.at[group], recv_sem=rsem.at[sem],
            device_id=to, device_id_type=MESH).start()
        return sem

    def same(ref, to, sem, group):
        return send(ref, ref, to, sem, group)

    def waiting(ref, sem, group):
        return pltpu.make_async_remote_copy(
            src_ref=ref, dst_ref=ref, send_sem=ssem.at[group], recv_sem=rsem.at[sem],
            device_id=sibling, device_id_type=MESH)

    def landed(sem, ref):
        waiting(ref, sem, 0).wait_recv()

    own_copy = pltpu.make_async_copy(occ_hbm, occ.at[zl, x, c], lsem.at[0])
    own_copy.start()
    ints_copy = pltpu.make_async_copy(ints_hbm, ints, lsem.at[1])
    ints_copy.start()

    barrier = pltpu.get_barrier_semaphore()
    partners = [sibling, at(dx=1), at(dx=2), at(dx=-1), at(dy=1), at(dy=-1), at(dz=1), at(dz=-1),
                at(dz=4), at(dz=-4), in_group(1), in_group(2), in_group(3)]
    for partner in partners:
        pl.semaphore_signal(barrier, inc=1, device_id=partner, device_id_type=MESH)
    pl.semaphore_wait(barrier, len(partners))
    own_copy.wait()

    xr, xl, xo = up(x, 1), up(x, -1), up(x, 2)
    zr, zd, zo = up(zl, 1), up(zl, -1), up(zl, 2)
    east, west, north, south = at(dx=1), at(dx=-1), at(dz=1), at(dz=-1)
    PA, PB = pl.ds(0, 256), pl.ds(256, 256)
    ALL, TOP, BOT = pl.ds(0, 192), pl.ds(0, 96), pl.ds(96, 96)

    def blk(bz, bx, rows, cols):
        return occ.at[bz, bx, c, rows, cols]

    GATHER, SIBLING, BLOCKS, SUMS = range(4)
    half_block = blk(zl, x, ALL, PA)

    def hop(ref, to, sem=None):
        return same(ref, to, arrival() if sem is None else sem, GATHER)

    def over(ref, sem):
        return same(ref, sibling, sem, SIBLING)

    sib_0, sib_1, sib_2 = arrival(), arrival(), arrival()
    fwd_a = [[], []]
    fwd_b = [[], []]
    own_a, own_b = blk(zl, x, ALL, PA), blk(zl, x, ALL, PB)
    a_e, a_w = hop(own_a, east), hop(own_a, west)
    b_n, b_s = hop(own_b, north), hop(own_b, south)
    fwd_a[0].append(hop(own_a, north))
    fwd_a[1].append(hop(own_a, south))
    fwd_b[0].append(hop(own_b, east))
    fwd_b[1].append(hop(own_b, west))
    over(occ.at[zl, x, c], sib_0)

    a_2, b_2 = arrival(), arrival()
    landed(a_e, half_block)
    hop(blk(zl, xl, TOP, PA), east, a_2)
    fwd_a[0].append(hop(blk(zl, xl, ALL, PA), north))
    fwd_a[1].append(hop(blk(zl, xl, ALL, PA), south))
    landed(b_n, half_block)
    hop(blk(zd, x, TOP, PB), north, b_2)
    fwd_b[0].append(hop(blk(zd, x, ALL, PB), east))
    fwd_b[1].append(hop(blk(zd, x, ALL, PB), west))
    landed(a_w, half_block)
    hop(blk(zl, xr, BOT, PA), west, a_2)
    fwd_a[0].append(hop(blk(zl, xr, ALL, PA), north))
    fwd_a[1].append(hop(blk(zl, xr, ALL, PA), south))
    landed(b_s, half_block)
    hop(blk(zr, x, BOT, PB), south, b_2)
    fwd_b[0].append(hop(blk(zr, x, ALL, PB), east))
    fwd_b[1].append(hop(blk(zr, x, ALL, PB), west))
    over(blk(zl, xl, ALL, PA), sib_0)
    over(blk(zl, xr, ALL, PA), sib_0)
    over(blk(zd, x, ALL, PB), sib_0)
    over(blk(zr, x, ALL, PB), sib_0)
    landed(a_2, half_block)
    fwd_a[0].append(hop(blk(zl, xo, ALL, PA), north))
    fwd_a[1].append(hop(blk(zl, xo, ALL, PA), south))
    over(blk(zl, xo, ALL, PA), sib_0)
    landed(b_2, half_block)
    fwd_b[0].append(hop(blk(zo, x, ALL, PB), east))
    fwd_b[1].append(hop(blk(zo, x, ALL, PB), west))
    over(blk(zo, x, ALL, PB), sib_0)

    last = []
    for bx, bz, j in zip((x, xl, xr, xo), (zl, zd, zr, zo), range(4)):
        last_a, last_b = arrival(), arrival()
        landed(fwd_a[0][j], half_block)
        hop(blk(zd, bx, TOP, PA), north, last_a)
        over(blk(zd, bx, ALL, PA), sib_1)
        landed(fwd_a[1][j], half_block)
        hop(blk(zr, bx, BOT, PA), south, last_a)
        over(blk(zr, bx, ALL, PA), sib_1)
        landed(fwd_b[0][j], half_block)
        hop(blk(bz, xl, TOP, PB), east, last_b)
        over(blk(bz, xl, ALL, PB), sib_1)
        landed(fwd_b[1][j], half_block)
        hop(blk(bz, xr, BOT, PB), west, last_b)
        over(blk(bz, xr, ALL, PB), sib_1)
        last.append((last_a, bx, last_b, bz))

    def lanes(start, size):
        return pl.ds(pl.multiple_of(start, 128), size)

    def part_a(bz):
        return jnp.dot(ints[:, lanes(bz * 1536, 1536)],
                       occ[bz, :, :, :, 0:256].reshape(1536, 256), preferred_element_type=F32)

    def part_b(bx):
        total = None
        for bz in range(4):
            term = jnp.dot(ints[:, lanes(bz * 1536 + bx * 384, 384)],
                           occ[bz, bx, :, :, 256:512].reshape(384, 256), preferred_element_type=F32)
            total = term if total is None else total + term
        return total

    ints_copy.wait()
    landed(sib_0, occ.at[zl, :, 1 - c])
    hacc[:, 0:256] = part_a(zl)
    hacc[:, 256:512] = part_b(x)
    for last_a, bx, last_b, bz in last:
        landed(last_a, half_block)
        over(blk(zo, bx, ALL, PA), sib_2)
        landed(last_b, half_block)
        over(blk(bz, xo, ALL, PB), sib_2)
    landed(sib_1, occ.at[zl])
    hacc[:, 0:256] += part_a(zd)
    hacc[:, 256:512] += part_b(xl)
    hacc[:, 0:256] += part_a(zr)
    hacc[:, 256:512] += part_b(xr)
    landed(sib_2, occ.at[zl, :, 1 - c])
    h_a = (hacc[:, 0:256] + part_a(zo)).astype(BF16)
    h_b = (hacc[:, 256:512] + part_b(xo)).astype(BF16)
    hrow[x, :, 0:256] = h_a
    hrow[x, :, 256:512] = h_b
    for s in range(3):
        hcol[s, zl, c, :, 0:256] = h_a[64 * s:64 * s + 64]
        hcol[s, zl, c, :, 256:512] = h_b[64 * s:64 * s + 64]

    def columns_out(s):
        sem = arrival()
        for d in (1, 3, 2):
            same(hcol.at[s, zl, c], in_group(d), sem, BLOCKS)
        return sem

    UPPER, LOWER = pl.ds(0, 96), pl.ds(96, 96)
    r_in = [arrival(), arrival()]
    c_in = []
    for t, half in enumerate((UPPER, LOWER)):
        for d in (2, 1, -1):
            same(hrow.at[x, half], at(dx=d), r_in[t], BLOCKS)
        c_in.append(columns_out(t))
    c_in.append(columns_out(2))
    c_sib = [arrival() for s in range(3)]
    for s in range(3):
        same(hcol.at[s, zl, c], sibling, c_sib[s], BLOCKS)

    yr, yl, yo = up(y, 1), up(y, -1), up(y, 2)
    y_up, y_dn = at(dy=1), at(dy=-1)
    hr, hl, ho = up(zh, 1), up(zh, -1), up(zh, 2)
    z_up, z_dn = at(dz=4), at(dz=-4)
    A, B = pl.ds(0, 192), pl.ds(192, 192)
    TA, TB = pl.ds(0, 48), pl.ds(48, 48)
    y1, y2, xs, z1, z2 = {}, {}, {}, {}, {}

    def columns_in(s):
        landed(c_in[s], hcol.at[s, 0:3, c])
        for d in (1, 3, 2):
            same(hcol.at[s, up(zl, d), c], sibling, c_sib[s], BLOCKS)
        landed(c_sib[s], hcol.at[s, :, 1 - c])

    def product(k):
        s, t = k // 2, k % 2
        rows = hrow[:, 96 * t:96 * t + 96].reshape(384, 512)
        for half in range(2):
            cols = hcol[s, 2 * half:2 * half + 2].reshape(256, 512)
            p = lax.dot_general(rows, cols, (((1,), (1,)), ((), ())), preferred_element_type=F32)
            p = p.astype(BF16)
            pb[k, 2 * half] = p[:, 0:128]
            pb[k, 2 * half + 1] = p[:, 128:256]

    def pass_on(src, dst, to, sem):
        send(src, dst, to, sem, SUMS)

    def y_first(k):
        if k % 2 == 0:
            columns_in(k // 2)
        if k < 2:
            landed(r_in[k], hrow.at[0:3, UPPER])
        product(k)
        y1[k], y2[k] = arrival(), arrival()
        pass_on(pb.at[k, yo, A], yin.at[k, 0], y_up, y1[k])
        pass_on(pb.at[k, yo, B], yin.at[k, 1], y_dn, y1[k])
        pass_on(pb.at[k, yr, B], yin.at[k, 2], y_up, y2[k])
        pass_on(pb.at[k, yl, A], yin.at[k, 3], y_dn, y2[k])

    def y_second(k):
        landed(y1[k], yin.at[k, 0:2])
        pb[k, yr, A] = (pb[k, yr, A].astype(F32) + yin[k, 0].astype(F32)).astype(BF16)
        pass_on(pb.at[k, yr, A], yin.at[k, 4], y_up, y2[k])
        pb[k, yl, B] = (pb[k, yl, B].astype(F32) + yin[k, 1].astype(F32)).astype(BF16)
        pass_on(pb.at[k, yl, B], yin.at[k, 5], y_dn, y2[k])

    def y_last(k):
        landed(y2[k], yin.at[k, 2:6])
        ysum[k, 0:2] = (pb[k, y, A].astype(F32) + yin[k, 3].astype(F32)
                        + yin[k, 4].astype(F32)).astype(BF16).reshape(2, 96, 128)
        ysum[k, 2:4] = (pb[k, y, B].astype(F32) + yin[k, 2].astype(F32)
                        + yin[k, 5].astype(F32)).astype(BF16).reshape(2, 96, 128)
        xs[k] = arrival()
        for d in (2, 1, -1):
            pass_on(ysum.at[k, up(x, d)], xin.at[k, x], at(dx=d), xs[k])
        xin[k, x] = ysum[k, x]

    def z_first(k):
        landed(xs[k], xin.at[k, 0:3])
        z1[k], z2[k] = arrival(), arrival()
        pass_on(xin.at[k, ho, TA], zin.at[k, 0], z_up, z1[k])
        pass_on(xin.at[k, ho, TB], zin.at[k, 1], z_dn, z1[k])
        pass_on(xin.at[k, hr, TB], zin.at[k, 2], z_up, z2[k])
        pass_on(xin.at[k, hl, TA], zin.at[k, 3], z_dn, z2[k])

    def z_second(k):
        landed(z1[k], zin.at[k, 0:2])
        zbuf[k, 0] = (xin[k, hr, TA].astype(F32) + zin[k, 0].astype(F32)).astype(BF16)
        pass_on(zbuf.at[k, 0], zin.at[k, 4], z_up, z2[k])
        zbuf[k, 1] = (xin[k, hl, TB].astype(F32) + zin[k, 1].astype(F32)).astype(BF16)
        pass_on(zbuf.at[k, 1], zin.at[k, 5], z_dn, z2[k])

    def z_last(k):
        landed(z2[k], zin.at[k, 2:6])
        top = xin[k, zh, TA].astype(F32) + zin[k, 3].astype(F32) + zin[k, 4].astype(F32)
        bot = xin[k, zh, TB].astype(F32) + zin[k, 2].astype(F32) + zin[k, 5].astype(F32)
        s, t = k // 2, k % 2
        for first, v in ((96 * t, top), (96 * t + 48, bot)):
            out_ref[first:first + 48, 64 * s:64 * s + 64] = v[:, 0:64]
            out_ref[first:first + 48, 192 + 64 * s:192 + 64 * s + 64] = v[:, 64:128]

    steps = {"F": y_first, "S": y_second, "L": y_last, "f": z_first, "s": z_second, "l": z_last}
    for part in ("F0F1S0F2S1F3L0S2F4L1S3f0F5L2f1S4", "L3s0S5f2L4s1f3L5s2f4f5l0",
                 "s3l1s4l2s5l3l4l5"):
        for j in range(0, len(part), 2):
            steps[part[j]](int(part[j + 1]))
    for group, ref in ((GATHER, occ.at[0:3, 0:3, :, 0:160]), (SIBLING, occ.at[:, :, 0]),
                       (BLOCKS, occ.at[0:3, :, 0, 0:160]), (SUMS, occ.at[0:3, 0:3, :, 0:144])):
        waiting(ref, 0, group).wait_send()
    assert made[0] == N_SEM, made[0]


def local(integrals, occupied):
    return pl.pallas_call(
        kernel,
        out_shape=jax.ShapeDtypeStruct((192, 384), F32),
        in_specs=[pl.BlockSpec(memory_space=pltpu.HBM)] * 2,
        out_specs=pl.BlockSpec(memory_space=pltpu.VMEM),
        scratch_shapes=[
            pltpu.VMEM((4, 4, 2, 192, 512), BF16),
            pltpu.VMEM((192, 6144), BF16),
            pltpu.VMEM((192, 512), F32),
            pltpu.VMEM((4, 192, 512), BF16),
            pltpu.VMEM((3, 4, 2, 64, 512), BF16),
            pltpu.VMEM((6, 4, 384, 128), BF16),
            pltpu.VMEM((6, 6, 192, 128), BF16),
            pltpu.VMEM((6, 4, 96, 128), BF16),
            pltpu.VMEM((6, 4, 96, 128), BF16),
            pltpu.VMEM((6, 6, 48, 128), BF16),
            pltpu.VMEM((6, 2, 48, 128), BF16),
            pltpu.SemaphoreType.DMA((4,)),
            pltpu.SemaphoreType.DMA((N_SEM,)),
            pltpu.SemaphoreType.DMA((2,)),
        ],
        compiler_params=pltpu.CompilerParams(
            collective_id=0, has_side_effects=True, vmem_limit_bytes=60 << 20),
        name="exchange",
    )(integrals.reshape(192, 6144), occupied)


def solution(mesh):
    in_specs = (P("grp", "row", None), P("row", None))
    return jax.shard_map(local, mesh=mesh, in_specs=in_specs, out_specs=P("row", "grp"), check_vma=False)
```

```python
import jax
import jax.numpy as jnp
from jax import lax
from jax.experimental import pallas as pl
from jax.experimental.pallas import tpu as pltpu
from jax.sharding import PartitionSpec as P

MESH = pl.DeviceIdType.MESH
F32 = jnp.float32
BF16 = jnp.bfloat16

N_SEM = 73


def kernel(ints_hbm, occ_hbm, out_ref, occ, ints, hacc, hrow, hcol, pb,
           yin, ysum, xin, zin, zbuf, ssem, rsem, lsem):
    grp, row = lax.axis_index("grp"), lax.axis_index("row")
    y, zh = grp // 4, grp % 4
    zl, x, c = row // 8, (row // 2) % 4, row % 2
    z = zh * 4 + zl

    def up(v, d, n=4):
        return (v + d + n) % n

    def at(dx=0, dy=0, dz=0):
        zz = up(z, dz, 16)
        return (up(y, dy) * 4 + zz // 4, (zz % 4) * 8 + up(x, dx) * 2 + c)

    def in_group(d):
        return (grp, up(zl, d) * 8 + x * 2 + c)

    sibling = (grp, zl * 8 + x * 2 + (1 - c))

    made = [0]

    def arrival():
        made[0] += 1
        return made[0] - 1

    def send(src, dst, to, sem, group):
        pltpu.make_async_remote_copy(
            src_ref=src, dst_ref=dst, send_sem=ssem.at[group], recv_sem=rsem.at[sem],
            device_id=to, device_id_type=MESH).start()
        return sem

    def same(ref, to, sem, group):
        return send(ref, ref, to, sem, group)

    def waiting(ref, sem, group):
        return pltpu.make_async_remote_copy(
            src_ref=ref, dst_ref=ref, send_sem=ssem.at[group], recv_sem=rsem.at[sem],
            device_id=sibling, device_id_type=MESH)

    def landed(sem, ref):
        waiting(ref, sem, 0).wait_recv()

    own_copy = pltpu.make_async_copy(occ_hbm, occ.at[zl, x, c], lsem.at[0])
    own_copy.start()
    ints_copy = pltpu.make_async_copy(ints_hbm, ints, lsem.at[1])
    ints_copy.start()

    barrier = pltpu.get_barrier_semaphore()
    partners = [sibling, at(dx=1), at(dx=2), at(dx=-1), at(dy=1), at(dy=-1), at(dz=1), at(dz=-1),
                at(dz=4), at(dz=-4), in_group(1), in_group(2), in_group(3)]
    for partner in partners:
        pl.semaphore_signal(barrier, inc=1, device_id=partner, device_id_type=MESH)
    pl.semaphore_wait(barrier, len(partners))
    own_copy.wait()

    xr, xl, xo = up(x, 1), up(x, -1), up(x, 2)
    zr, zd, zo = up(zl, 1), up(zl, -1), up(zl, 2)
    east, west, north, south = at(dx=1), at(dx=-1), at(dz=1), at(dz=-1)
    PA, PB = pl.ds(0, 256), pl.ds(256, 256)
    ALL, TOP, BOT = pl.ds(0, 192), pl.ds(0, 96), pl.ds(96, 96)

    def blk(bz, bx, rows, cols):
        return occ.at[bz, bx, c, rows, cols]

    GATHER, SIBLING, BLOCKS, SUMS = range(4)
    half_block = blk(zl, x, ALL, PA)

    def hop(ref, to, sem=None):
        return same(ref, to, arrival() if sem is None else sem, GATHER)

    def over(ref, sem):
        return same(ref, sibling, sem, SIBLING)

    sib_0, sib_1, sib_2 = arrival(), arrival(), arrival()
    fwd_a = [[], []]
    fwd_b = [[], []]
    own_a, own_b = blk(zl, x, ALL, PA), blk(zl, x, ALL, PB)
    a_e, a_w = hop(own_a, east), hop(own_a, west)
    b_n, b_s = hop(own_b, north), hop(own_b, south)
    fwd_a[0].append(hop(own_a, north))
    fwd_a[1].append(hop(own_a, south))
    fwd_b[0].append(hop(own_b, east))
    fwd_b[1].append(hop(own_b, west))
    over(occ.at[zl, x, c], sib_0)

    a_2, b_2 = arrival(), arrival()
    landed(a_e, half_block)
    hop(blk(zl, xl, TOP, PA), east, a_2)
    fwd_a[0].append(hop(blk(zl, xl, ALL, PA), north))
    fwd_a[1].append(hop(blk(zl, xl, ALL, PA), south))
    landed(b_n, half_block)
    hop(blk(zd, x, TOP, PB), north, b_2)
    fwd_b[0].append(hop(blk(zd, x, ALL, PB), east))
    fwd_b[1].append(hop(blk(zd, x, ALL, PB), west))
    landed(a_w, half_block)
    hop(blk(zl, xr, BOT, PA), west, a_2)
    fwd_a[0].append(hop(blk(zl, xr, ALL, PA), north))
    fwd_a[1].append(hop(blk(zl, xr, ALL, PA), south))
    landed(b_s, half_block)
    hop(blk(zr, x, BOT, PB), south, b_2)
    fwd_b[0].append(hop(blk(zr, x, ALL, PB), east))
    fwd_b[1].append(hop(blk(zr, x, ALL, PB), west))
    over(blk(zl, xl, ALL, PA), sib_0)
    over(blk(zl, xr, ALL, PA), sib_0)
    over(blk(zd, x, ALL, PB), sib_0)
    over(blk(zr, x, ALL, PB), sib_0)
    landed(a_2, half_block)
    fwd_a[0].append(hop(blk(zl, xo, ALL, PA), north))
    fwd_a[1].append(hop(blk(zl, xo, ALL, PA), south))
    over(blk(zl, xo, ALL, PA), sib_0)
    landed(b_2, half_block)
    fwd_b[0].append(hop(blk(zo, x, ALL, PB), east))
    fwd_b[1].append(hop(blk(zo, x, ALL, PB), west))
    over(blk(zo, x, ALL, PB), sib_0)

    last = []
    for bx, bz, j in zip((x, xl, xr, xo), (zl, zd, zr, zo), range(4)):
        last_a, last_b = arrival(), arrival()
        landed(fwd_a[0][j], half_block)
        hop(blk(zd, bx, TOP, PA), north, last_a)
        over(blk(zd, bx, ALL, PA), sib_1)
        landed(fwd_a[1][j], half_block)
        hop(blk(zr, bx, BOT, PA), south, last_a)
        over(blk(zr, bx, ALL, PA), sib_1)
        landed(fwd_b[0][j], half_block)
        hop(blk(bz, xl, TOP, PB), east, last_b)
        over(blk(bz, xl, ALL, PB), sib_1)
        landed(fwd_b[1][j], half_block)
        hop(blk(bz, xr, BOT, PB), west, last_b)
        over(blk(bz, xr, ALL, PB), sib_1)
        last.append((last_a, bx, last_b, bz))

    def lanes(start, size):
        return pl.ds(pl.multiple_of(start, 128), size)

    def part_a(bz):
        return jnp.dot(ints[:, lanes(bz * 1536, 1536)],
                       occ[bz, :, :, :, 0:256].reshape(1536, 256), preferred_element_type=F32)

    def part_b(bx):
        total = None
        for bz in range(4):
            term = jnp.dot(ints[:, lanes(bz * 1536 + bx * 384, 384)],
                           occ[bz, bx, :, :, 256:512].reshape(384, 256), preferred_element_type=F32)
            total = term if total is None else total + term
        return total

    ints_copy.wait()
    landed(sib_0, occ.at[zl, :, 1 - c])
    hacc[:, 0:256] = part_a(zl)
    hacc[:, 256:512] = part_b(x)
    for last_a, bx, last_b, bz in last:
        landed(last_a, half_block)
        over(blk(zo, bx, ALL, PA), sib_2)
        landed(last_b, half_block)
        over(blk(bz, xo, ALL, PB), sib_2)
    landed(sib_1, occ.at[zl])
    hacc[:, 0:256] += part_a(zd)
    hacc[:, 256:512] += part_b(xl)
    hacc[:, 0:256] += part_a(zr)
    hacc[:, 256:512] += part_b(xr)
    landed(sib_2, occ.at[zl, :, 1 - c])
    h_a = (hacc[:, 0:256] + part_a(zo)).astype(BF16)
    h_b = (hacc[:, 256:512] + part_b(xo)).astype(BF16)
    hrow[x, :, 0:256] = h_a
    hrow[x, :, 256:512] = h_b
    for s in range(3):
        hcol[s, zl, c, :, 0:256] = h_a[64 * s:64 * s + 64]
        hcol[s, zl, c, :, 256:512] = h_b[64 * s:64 * s + 64]

    def columns_out(s):
        sem = arrival()
        for d in (1, 3, 2):
            same(hcol.at[s, zl, c], in_group(d), sem, BLOCKS)
        return sem

    Q = [pl.ds(48 * j, 48) for j in range(4)]
    r_1, r_2 = [arrival(), arrival()], [arrival(), arrival()]
    same(hrow.at[x, TOP], east, r_1[0], BLOCKS)
    same(hrow.at[x, TOP], west, r_1[0], BLOCKS)
    c_in = [columns_out(0)]
    same(hrow.at[x, BOT], east, r_1[1], BLOCKS)
    same(hrow.at[x, BOT], west, r_1[1], BLOCKS)
    c_in += [columns_out(1), columns_out(2)]
    c_sib = [arrival() for s in range(3)]
    for s in range(3):
        same(hcol.at[s, zl, c], sibling, c_sib[s], BLOCKS)
    for t in range(2):
        landed(r_1[t], hrow.at[x])
        same(hrow.at[xl, Q[2 * t]], east, r_2[t], BLOCKS)
        same(hrow.at[xr, Q[2 * t + 1]], west, r_2[t], BLOCKS)

    yr, yl, yo = up(y, 1), up(y, -1), up(y, 2)
    y_up, y_dn = at(dy=1), at(dy=-1)
    hr, hl, ho = up(zh, 1), up(zh, -1), up(zh, 2)
    z_up, z_dn = at(dz=4), at(dz=-4)
    A, B = pl.ds(0, 192), pl.ds(192, 192)
    TA, TB = pl.ds(0, 48), pl.ds(48, 48)
    y1, y2, xs, z1, z2 = {}, {}, {}, {}, {}

    def columns_in(s):
        landed(c_in[s], hcol.at[s, 0:3, c])
        for d in (1, 3, 2):
            same(hcol.at[s, up(zl, d), c], sibling, c_sib[s], BLOCKS)
        landed(c_sib[s], hcol.at[s, :, 1 - c])

    def product(k):
        s, t = k // 2, k % 2
        rows = hrow[:, 96 * t:96 * t + 96].reshape(384, 512)
        for half in range(2):
            cols = hcol[s, 2 * half:2 * half + 2].reshape(256, 512)
            p = lax.dot_general(rows, cols, (((1,), (1,)), ((), ())), preferred_element_type=F32)
            p = p.astype(BF16)
            pb[k, 2 * half] = p[:, 0:128]
            pb[k, 2 * half + 1] = p[:, 128:256]

    def pass_on(src, dst, to, sem):
        send(src, dst, to, sem, SUMS)

    def y_first(k):
        if k % 2 == 0:
            columns_in(k // 2)
        if k < 2:
            landed(r_2[k], hrow.at[x, TOP])
        product(k)
        y1[k], y2[k] = arrival(), arrival()
        pass_on(pb.at[k, yo, A], yin.at[k, 0], y_up, y1[k])
        pass_on(pb.at[k, yo, B], yin.at[k, 1], y_dn, y1[k])
        pass_on(pb.at[k, yr, B], yin.at[k, 2], y_up, y2[k])
        pass_on(pb.at[k, yl, A], yin.at[k, 3], y_dn, y2[k])

    def y_second(k):
        landed(y1[k], yin.at[k, 0:2])
        pb[k, yr, A] = (pb[k, yr, A].astype(F32) + yin[k, 0].astype(F32)).astype(BF16)
        pass_on(pb.at[k, yr, A], yin.at[k, 4], y_up, y2[k])
        pb[k, yl, B] = (pb[k, yl, B].astype(F32) + yin[k, 1].astype(F32)).astype(BF16)
        pass_on(pb.at[k, yl, B], yin.at[k, 5], y_dn, y2[k])

    def y_last(k):
        landed(y2[k], yin.at[k, 2:6])
        ysum[k, 0:2] = (pb[k, y, A].astype(F32) + yin[k, 3].astype(F32)
                        + yin[k, 4].astype(F32)).astype(BF16).reshape(2, 96, 128)
        ysum[k, 2:4] = (pb[k, y, B].astype(F32) + yin[k, 2].astype(F32)
                        + yin[k, 5].astype(F32)).astype(BF16).reshape(2, 96, 128)
        xs[k] = arrival()
        for d in (2, 1, -1):
            pass_on(ysum.at[k, up(x, d)], xin.at[k, x], at(dx=d), xs[k])
        xin[k, x] = ysum[k, x]

    def z_first(k):
        landed(xs[k], xin.at[k, 0:3])
        z1[k], z2[k] = arrival(), arrival()
        pass_on(xin.at[k, ho, TA], zin.at[k, 0], z_up, z1[k])
        pass_on(xin.at[k, ho, TB], zin.at[k, 1], z_dn, z1[k])
        pass_on(xin.at[k, hr, TB], zin.at[k, 2], z_up, z2[k])
        pass_on(xin.at[k, hl, TA], zin.at[k, 3], z_dn, z2[k])

    def z_second(k):
        landed(z1[k], zin.at[k, 0:2])
        zbuf[k, 0] = (xin[k, hr, TA].astype(F32) + zin[k, 0].astype(F32)).astype(BF16)
        pass_on(zbuf.at[k, 0], zin.at[k, 4], z_up, z2[k])
        zbuf[k, 1] = (xin[k, hl, TB].astype(F32) + zin[k, 1].astype(F32)).astype(BF16)
        pass_on(zbuf.at[k, 1], zin.at[k, 5], z_dn, z2[k])

    def z_last(k):
        landed(z2[k], zin.at[k, 2:6])
        top = xin[k, zh, TA].astype(F32) + zin[k, 3].astype(F32) + zin[k, 4].astype(F32)
        bot = xin[k, zh, TB].astype(F32) + zin[k, 2].astype(F32) + zin[k, 5].astype(F32)
        s, t = k // 2, k % 2
        for first, v in ((96 * t, top), (96 * t + 48, bot)):
            out_ref[first:first + 48, 64 * s:64 * s + 64] = v[:, 0:64]
            out_ref[first:first + 48, 192 + 64 * s:192 + 64 * s + 64] = v[:, 64:128]

    steps = {"F": y_first, "S": y_second, "L": y_last, "f": z_first, "s": z_second, "l": z_last}
    for part in ("F0F1S0F2S1F3L0S2F4L1S3f0F5L2f1S4", "L3s0S5f2L4s1f3L5s2f4f5l0",
                 "s3l1s4l2s5l3l4l5"):
        for j in range(0, len(part), 2):
            steps[part[j]](int(part[j + 1]))
    for group, ref in ((GATHER, occ.at[0:3, 0:3, :, 0:160]), (SIBLING, occ.at[:, :, 0]),
                       (BLOCKS, occ.at[0:3, :, 0, 0:160]), (SUMS, occ.at[0:3, 0:3, :, 0:144])):
        waiting(ref, 0, group).wait_send()
    assert made[0] == N_SEM, made[0]


def local(integrals, occupied):
    return pl.pallas_call(
        kernel,
        out_shape=jax.ShapeDtypeStruct((192, 384), F32),
        in_specs=[pl.BlockSpec(memory_space=pltpu.HBM)] * 2,
        out_specs=pl.BlockSpec(memory_space=pltpu.VMEM),
        scratch_shapes=[
            pltpu.VMEM((4, 4, 2, 192, 512), BF16),
            pltpu.VMEM((192, 6144), BF16),
            pltpu.VMEM((192, 512), F32),
            pltpu.VMEM((4, 192, 512), BF16),
            pltpu.VMEM((3, 4, 2, 64, 512), BF16),
            pltpu.VMEM((6, 4, 384, 128), BF16),
            pltpu.VMEM((6, 6, 192, 128), BF16),
            pltpu.VMEM((6, 4, 96, 128), BF16),
            pltpu.VMEM((6, 4, 96, 128), BF16),
            pltpu.VMEM((6, 6, 48, 128), BF16),
            pltpu.VMEM((6, 2, 48, 128), BF16),
            pltpu.SemaphoreType.DMA((4,)),
            pltpu.SemaphoreType.DMA((N_SEM,)),
            pltpu.SemaphoreType.DMA((2,)),
        ],
        compiler_params=pltpu.CompilerParams(
            collective_id=0, has_side_effects=True, vmem_limit_bytes=60 << 20),
        name="exchange",
    )(integrals.reshape(192, 6144), occupied)


def solution(mesh):
    in_specs = (P("grp", "row", None), P("row", None))
    return jax.shard_map(local, mesh=mesh, in_specs=in_specs, out_specs=P("row", "grp"), check_vma=False)
```

```python
import jax
import jax.numpy as jnp
from jax import lax
from jax.experimental import pallas as pl
from jax.experimental.pallas import tpu as pltpu
from jax.sharding import PartitionSpec as P

MESH = pl.DeviceIdType.MESH
F32 = jnp.float32
BF16 = jnp.bfloat16

N_SEM = 73


def kernel(ints_hbm, occ_hbm, out_ref, occ, ints, hacc, hrow, hcol, pb,
           yin, ysum, xin, zin, zbuf, ssem, rsem, lsem):
    grp, row = lax.axis_index("grp"), lax.axis_index("row")
    y, zh = grp // 4, grp % 4
    zl, x, c = row // 8, (row // 2) % 4, row % 2
    z = zh * 4 + zl

    def up(v, d, n=4):
        return (v + d + n) % n

    def at(dx=0, dy=0, dz=0):
        zz = up(z, dz, 16)
        return (up(y, dy) * 4 + zz // 4, (zz % 4) * 8 + up(x, dx) * 2 + c)

    def in_group(d):
        return (grp, up(zl, d) * 8 + x * 2 + c)

    sibling = (grp, zl * 8 + x * 2 + (1 - c))

    made = [0]

    def arrival():
        made[0] += 1
        return made[0] - 1

    def send(src, dst, to, sem, group):
        pltpu.make_async_remote_copy(
            src_ref=src, dst_ref=dst, send_sem=ssem.at[group], recv_sem=rsem.at[sem],
            device_id=to, device_id_type=MESH).start()
        return sem

    def same(ref, to, sem, group):
        return send(ref, ref, to, sem, group)

    def waiting(ref, sem, group):
        return pltpu.make_async_remote_copy(
            src_ref=ref, dst_ref=ref, send_sem=ssem.at[group], recv_sem=rsem.at[sem],
            device_id=sibling, device_id_type=MESH)

    def landed(sem, ref):
        waiting(ref, sem, 0).wait_recv()

    own_copy = pltpu.make_async_copy(occ_hbm, occ.at[zl, x, c], lsem.at[0])
    own_copy.start()
    ints_copy = pltpu.make_async_copy(ints_hbm, ints, lsem.at[1])
    ints_copy.start()

    barrier = pltpu.get_barrier_semaphore()
    partners = [sibling, at(dx=1), at(dx=2), at(dx=-1), at(dy=1), at(dy=-1), at(dz=1), at(dz=-1),
                at(dz=4), at(dz=-4), in_group(1), in_group(2), in_group(3)]
    for partner in partners:
        pl.semaphore_signal(barrier, inc=1, device_id=partner, device_id_type=MESH)
    pl.semaphore_wait(barrier, len(partners))
    own_copy.wait()

    xr, xl, xo = up(x, 1), up(x, -1), up(x, 2)
    zr, zd, zo = up(zl, 1), up(zl, -1), up(zl, 2)
    east, west, north, south = at(dx=1), at(dx=-1), at(dz=1), at(dz=-1)
    PA, PB = pl.ds(0, 256), pl.ds(256, 256)
    ALL, TOP, BOT = pl.ds(0, 192), pl.ds(0, 96), pl.ds(96, 96)

    def blk(bz, bx, rows, cols):
        return occ.at[bz, bx, c, rows, cols]

    GATHER, SIBLING, BLOCKS, SUMS = range(4)
    half_block = blk(zl, x, ALL, PA)

    def hop(ref, to, sem=None):
        return same(ref, to, arrival() if sem is None else sem, GATHER)

    def over(ref, sem):
        return same(ref, sibling, sem, SIBLING)

    sib_0, sib_1, sib_2 = arrival(), arrival(), arrival()
    fwd_a = [[], []]
    fwd_b = [[], []]
    own_a, own_b = blk(zl, x, ALL, PA), blk(zl, x, ALL, PB)
    a_e, a_w = hop(own_a, east), hop(own_a, west)
    b_n, b_s = hop(own_b, north), hop(own_b, south)
    fwd_a[0].append(hop(own_a, north))
    fwd_a[1].append(hop(own_a, south))
    fwd_b[0].append(hop(own_b, east))
    fwd_b[1].append(hop(own_b, west))
    over(occ.at[zl, x, c], sib_0)

    a_2, b_2 = arrival(), arrival()
    landed(a_e, half_block)
    hop(blk(zl, xl, TOP, PA), east, a_2)
    fwd_a[0].append(hop(blk(zl, xl, ALL, PA), north))
    fwd_a[1].append(hop(blk(zl, xl, ALL, PA), south))
    landed(b_n, half_block)
    hop(blk(zd, x, TOP, PB), north, b_2)
    fwd_b[0].append(hop(blk(zd, x, ALL, PB), east))
    fwd_b[1].append(hop(blk(zd, x, ALL, PB), west))
    landed(a_w, half_block)
    hop(blk(zl, xr, BOT, PA), west, a_2)
    fwd_a[0].append(hop(blk(zl, xr, ALL, PA), north))
    fwd_a[1].append(hop(blk(zl, xr, ALL, PA), south))
    landed(b_s, half_block)
    hop(blk(zr, x, BOT, PB), south, b_2)
    fwd_b[0].append(hop(blk(zr, x, ALL, PB), east))
    fwd_b[1].append(hop(blk(zr, x, ALL, PB), west))
    over(blk(zl, xl, ALL, PA), sib_0)
    over(blk(zl, xr, ALL, PA), sib_0)
    over(blk(zd, x, ALL, PB), sib_0)
    over(blk(zr, x, ALL, PB), sib_0)
    landed(a_2, half_block)
    fwd_a[0].append(hop(blk(zl, xo, ALL, PA), north))
    fwd_a[1].append(hop(blk(zl, xo, ALL, PA), south))
    over(blk(zl, xo, ALL, PA), sib_0)
    landed(b_2, half_block)
    fwd_b[0].append(hop(blk(zo, x, ALL, PB), east))
    fwd_b[1].append(hop(blk(zo, x, ALL, PB), west))
    over(blk(zo, x, ALL, PB), sib_0)

    last = []
    for bx, bz, j in zip((x, xl, xr, xo), (zl, zd, zr, zo), range(4)):
        last_a, last_b = arrival(), arrival()
        landed(fwd_a[0][j], half_block)
        hop(blk(zd, bx, TOP, PA), north, last_a)
        over(blk(zd, bx, ALL, PA), sib_1)
        landed(fwd_a[1][j], half_block)
        hop(blk(zr, bx, BOT, PA), south, last_a)
        over(blk(zr, bx, ALL, PA), sib_1)
        landed(fwd_b[0][j], half_block)
        hop(blk(bz, xl, TOP, PB), east, last_b)
        over(blk(bz, xl, ALL, PB), sib_1)
        landed(fwd_b[1][j], half_block)
        hop(blk(bz, xr, BOT, PB), west, last_b)
        over(blk(bz, xr, ALL, PB), sib_1)
        last.append((last_a, bx, last_b, bz))

    def lanes(start, size):
        return pl.ds(pl.multiple_of(start, 128), size)

    def part_a(bz):
        return jnp.dot(ints[:, lanes(bz * 1536, 1536)],
                       occ[bz, :, :, :, 0:256].reshape(1536, 256), preferred_element_type=F32)

    def part_b(bx):
        total = None
        for bz in range(4):
            term = jnp.dot(ints[:, lanes(bz * 1536 + bx * 384, 384)],
                           occ[bz, bx, :, :, 256:512].reshape(384, 256), preferred_element_type=F32)
            total = term if total is None else total + term
        return total

    ints_copy.wait()
    landed(sib_0, occ.at[zl, :, 1 - c])
    hacc[:, 0:256] = part_a(zl)
    hacc[:, 256:512] = part_b(x)
    for last_a, bx, last_b, bz in last:
        landed(last_a, half_block)
        over(blk(zo, bx, ALL, PA), sib_2)
        landed(last_b, half_block)
        over(blk(bz, xo, ALL, PB), sib_2)
    landed(sib_1, occ.at[zl])
    hacc[:, 0:256] += part_a(zd)
    hacc[:, 256:512] += part_b(xl)
    hacc[:, 0:256] += part_a(zr)
    hacc[:, 256:512] += part_b(xr)
    landed(sib_2, occ.at[zl, :, 1 - c])
    h_a = (hacc[:, 0:256] + part_a(zo)).astype(BF16)
    h_b = (hacc[:, 256:512] + part_b(xo)).astype(BF16)
    hrow[x, :, 0:256] = h_a
    hrow[x, :, 256:512] = h_b
    for s in range(3):
        hcol[s, zl, c, :, 0:256] = h_a[64 * s:64 * s + 64]
        hcol[s, zl, c, :, 256:512] = h_b[64 * s:64 * s + 64]

    def columns_out(s):
        sem = arrival()
        for d in (1, 3, 2):
            same(hcol.at[s, zl, c], in_group(d), sem, BLOCKS)
        return sem

    Q = [pl.ds(48 * j, 48) for j in range(4)]
    r_1, r_2 = [arrival(), arrival()], [arrival(), arrival()]
    same(hrow.at[x, TOP], east, r_1[0], BLOCKS)
    same(hrow.at[x, TOP], west, r_1[0], BLOCKS)
    c_in = [columns_out(0)]
    same(hrow.at[x, BOT], east, r_1[1], BLOCKS)
    same(hrow.at[x, BOT], west, r_1[1], BLOCKS)
    c_in += [columns_out(1), columns_out(2)]
    c_sib = [arrival() for s in range(3)]
    for s in range(3):
        same(hcol.at[s, zl, c], sibling, c_sib[s], BLOCKS)
    for t in range(2):
        landed(r_1[t], hrow.at[x])
        same(hrow.at[xl, Q[2 * t]], east, r_2[t], BLOCKS)
        same(hrow.at[xr, Q[2 * t + 1]], west, r_2[t], BLOCKS)

    yr, yl, yo = up(y, 1), up(y, -1), up(y, 2)
    y_up, y_dn = at(dy=1), at(dy=-1)
    hr, hl, ho = up(zh, 1), up(zh, -1), up(zh, 2)
    z_up, z_dn = at(dz=4), at(dz=-4)
    A, B = pl.ds(0, 192), pl.ds(192, 192)
    TA, TB = pl.ds(0, 48), pl.ds(48, 48)
    y1, y2, xs, z1, z2 = {}, {}, {}, {}, {}

    def columns_in(s):
        landed(c_in[s], hcol.at[s, 0:3, c])
        for d in (1, 3, 2):
            same(hcol.at[s, up(zl, d), c], sibling, c_sib[s], BLOCKS)

    def product(k):
        s, t = k // 2, k % 2
        rows = hrow[:, 96 * t:96 * t + 96].reshape(384, 512)
        for half in range(2):
            cols = hcol[s, 2 * half:2 * half + 2].reshape(256, 512)
            p = lax.dot_general(rows, cols, (((1,), (1,)), ((), ())), preferred_element_type=F32)
            p = p.astype(BF16)
            pb[k, 2 * half] = p[:, 0:128]
            pb[k, 2 * half + 1] = p[:, 128:256]

    def pass_on(src, dst, to, sem):
        send(src, dst, to, sem, SUMS)

    def y_first(k):
        if k % 2 == 0:
            landed(c_sib[k // 2], hcol.at[k // 2, :, 1 - c])
        if k < 2:
            landed(r_2[k], hrow.at[x, TOP])
        product(k)
        y1[k], y2[k] = arrival(), arrival()
        pass_on(pb.at[k, yo, A], yin.at[k, 0], y_up, y1[k])
        pass_on(pb.at[k, yo, B], yin.at[k, 1], y_dn, y1[k])
        pass_on(pb.at[k, yr, B], yin.at[k, 2], y_up, y2[k])
        pass_on(pb.at[k, yl, A], yin.at[k, 3], y_dn, y2[k])

    def y_second(k):
        landed(y1[k], yin.at[k, 0:2])
        pb[k, yr, A] = (pb[k, yr, A].astype(F32) + yin[k, 0].astype(F32)).astype(BF16)
        pass_on(pb.at[k, yr, A], yin.at[k, 4], y_up, y2[k])
        pb[k, yl, B] = (pb[k, yl, B].astype(F32) + yin[k, 1].astype(F32)).astype(BF16)
        pass_on(pb.at[k, yl, B], yin.at[k, 5], y_dn, y2[k])

    def y_last(k):
        landed(y2[k], yin.at[k, 2:6])
        ysum[k, 0:2] = (pb[k, y, A].astype(F32) + yin[k, 3].astype(F32)
                        + yin[k, 4].astype(F32)).astype(BF16).reshape(2, 96, 128)
        ysum[k, 2:4] = (pb[k, y, B].astype(F32) + yin[k, 2].astype(F32)
                        + yin[k, 5].astype(F32)).astype(BF16).reshape(2, 96, 128)
        xs[k] = arrival()
        for d in (2, 1, -1):
            pass_on(ysum.at[k, up(x, d)], xin.at[k, x], at(dx=d), xs[k])
        xin[k, x] = ysum[k, x]

    def z_first(k):
        landed(xs[k], xin.at[k, 0:3])
        z1[k], z2[k] = arrival(), arrival()
        pass_on(xin.at[k, ho, TA], zin.at[k, 0], z_up, z1[k])
        pass_on(xin.at[k, ho, TB], zin.at[k, 1], z_dn, z1[k])
        pass_on(xin.at[k, hr, TB], zin.at[k, 2], z_up, z2[k])
        pass_on(xin.at[k, hl, TA], zin.at[k, 3], z_dn, z2[k])

    def z_second(k):
        landed(z1[k], zin.at[k, 0:2])
        zbuf[k, 0] = (xin[k, hr, TA].astype(F32) + zin[k, 0].astype(F32)).astype(BF16)
        pass_on(zbuf.at[k, 0], zin.at[k, 4], z_up, z2[k])
        zbuf[k, 1] = (xin[k, hl, TB].astype(F32) + zin[k, 1].astype(F32)).astype(BF16)
        pass_on(zbuf.at[k, 1], zin.at[k, 5], z_dn, z2[k])

    def z_last(k):
        landed(z2[k], zin.at[k, 2:6])
        top = xin[k, zh, TA].astype(F32) + zin[k, 3].astype(F32) + zin[k, 4].astype(F32)
        bot = xin[k, zh, TB].astype(F32) + zin[k, 2].astype(F32) + zin[k, 5].astype(F32)
        s, t = k // 2, k % 2
        for first, v in ((96 * t, top), (96 * t + 48, bot)):
            out_ref[first:first + 48, 64 * s:64 * s + 64] = v[:, 0:64]
            out_ref[first:first + 48, 192 + 64 * s:192 + 64 * s + 64] = v[:, 64:128]

    steps = {"C": columns_in, "F": y_first, "S": y_second, "L": y_last, "f": z_first, "s": z_second, "l": z_last}
    for part in ("C0F0F1S0C1F2S1F3L0S2C2L1F4f0S3F5L2f1S4L3", "s0S5f2L4s1f3L5s2f4f5l0s3l1s4l2s5l3l4l5"):
        for j in range(0, len(part), 2):
            steps[part[j]](int(part[j + 1]))
    for group, ref in ((GATHER, occ.at[0:3, 0:3, :, 0:160]), (SIBLING, occ.at[:, :, 0]),
                       (BLOCKS, occ.at[0:3, :, 0, 0:160]), (SUMS, occ.at[0:3, 0:3, :, 0:144])):
        waiting(ref, 0, group).wait_send()
    assert made[0] == N_SEM, made[0]


def local(integrals, occupied):
    return pl.pallas_call(
        kernel,
        out_shape=jax.ShapeDtypeStruct((192, 384), F32),
        in_specs=[pl.BlockSpec(memory_space=pltpu.HBM)] * 2,
        out_specs=pl.BlockSpec(memory_space=pltpu.VMEM),
        scratch_shapes=[
            pltpu.VMEM((4, 4, 2, 192, 512), BF16),
            pltpu.VMEM((192, 6144), BF16),
            pltpu.VMEM((192, 512), F32),
            pltpu.VMEM((4, 192, 512), BF16),
            pltpu.VMEM((3, 4, 2, 64, 512), BF16),
            pltpu.VMEM((6, 4, 384, 128), BF16),
            pltpu.VMEM((6, 6, 192, 128), BF16),
            pltpu.VMEM((6, 4, 96, 128), BF16),
            pltpu.VMEM((6, 4, 96, 128), BF16),
            pltpu.VMEM((6, 6, 48, 128), BF16),
            pltpu.VMEM((6, 2, 48, 128), BF16),
            pltpu.SemaphoreType.DMA((4,)),
            pltpu.SemaphoreType.DMA((N_SEM,)),
            pltpu.SemaphoreType.DMA((2,)),
        ],
        compiler_params=pltpu.CompilerParams(
            collective_id=0, has_side_effects=True, vmem_limit_bytes=60 << 20),
        name="exchange",
    )(integrals.reshape(192, 6144), occupied)


def solution(mesh):
    in_specs = (P("grp", "row", None), P("row", None))
    return jax.shard_map(local, mesh=mesh, in_specs=in_specs, out_specs=P("row", "grp"), check_vma=False)
```
